32 devices in a mesh: group: 2 (over y), section: 4 (over z), span: 2 (over x), mp: 2 (over core).
Axes of the slice: x: 2, y: 2, z: 4, core: 2. Of those that a mesh axis runs over, the one named last changes fastest.
Arguments:
- queries: bfloat16 [8, 256, 4096], P(('group', 'section'), None, ('span', 'mp')), parts along dimension 0, may hold values from -5 to 5
- keys_values: bfloat16 [2, 8, 256, 4096], P(None, ('group', 'section'), None, ('span', 'mp')), parts along dimension 1, may hold values from -5 to 5
- latents: bfloat16 [8, 256, 5120], P(('group', 'section'), ('span', 'mp')), parts along dimension 0, may hold values from -6 to 6
- out_weight: bfloat16 [4096, 5120], P(('span', 'mp')), may hold values from -3 to 3
- gate_table: float32 [8, 5120], replicated, may hold values from 0.5 to 1.5
- level_index: int32 [8], P(('group', 'section')), parts along dimension 0, may hold values from 0 to 7
- pair_window: int32 [6], P('group'), parts along dimension 0, may hold values from 0 to 256
Outputs:
- shifted: bfloat16 [8, 256, 5120], P(('group', 'section'), ('span', 'mp')), parts along dimension 0
The draws below stay inside these ranges and needn't reach their ends.
There are 2 independent parts, one for each index of `group`. The reference program is written for one: setup_inputs(seed, part) draws one part's arguments, and reference() takes and returns one part's arrays. A program takes and returns all parts, laid end to end along the dimension named above; an argument that names none is the same for every part. Nothing has to cross between parts.
All inputs are finite; a program needn't handle non-finite values.
Results may differ from the reference program's by a relative error of at most 0.015.
Values may be sent and summed in bfloat16 or wider, within the bound.
No kernel may reach another device: no remote copies, remote signals or barrier semaphores. Data moves between devices by JAX's collectives and lax.ppermute only.
A program may use at most 64 MiB of HBM per device.

```python
import math
import jax
import jax.numpy as jnp
from jax import lax

D = 5120
HD = 128
LEVELS = 8
SPAN_TOK = 256
NS = 4
HQ = 4096


def draw_triple(key):
    key_query, key_keys, key_values = jax.random.split(jax.random.fold_in(key, 7), 3)
    full_shape = (NS, SPAN_TOK, HQ)
    query_draw = jnp.clip(jax.random.normal(key_query, full_shape, jnp.float32), -5.0, 5.0)
    keys_draw = jnp.clip(jax.random.normal(key_keys, full_shape, jnp.float32), -5.0, 5.0)
    values_draw = jnp.clip(jax.random.normal(key_values, full_shape, jnp.float32), -5.0, 5.0)
    return (query_draw, keys_draw, values_draw)


def draw_queries(key, part):
    return draw_triple(key)[0].astype(jnp.bfloat16)


def draw_keys_values(key, part):
    triple = draw_triple(key)
    return jnp.stack([triple[1], triple[2]], 0).astype(jnp.bfloat16)


def draw_pair_window(key, part):
    key_rows, key_spot = jax.random.split(jax.random.fold_in(key, 11), 2)
    pair_count = NS - 1
    widths = jax.random.randint(key_rows, (pair_count,), 0, SPAN_TOK + 1)
    spot = jax.random.randint(key_spot, (), 0, pair_count)
    other = (spot + 1) % pair_count
    places = jnp.arange(pair_count, dtype=jnp.int32)
    widths = jnp.where(places == spot, SPAN_TOK, widths)
    widths = jnp.where(places == other, 0, widths)
    return widths.astype(jnp.int32)


def with_ends(values, rng, smallest, top_value):
    dims = values.shape
    index_at = [jax.random.randint(jax.random.fold_in(rng, axis), (), 0, dims[axis]) for axis in range(len(dims))]
    values = values.at[tuple(index_at)].set(smallest)
    longest = dims.index(max(dims))
    index_at[longest] = (index_at[longest] + 1) % dims[longest]
    return values.at[tuple(index_at)].set(top_value)


def block_scale(own_key, dims, pieces, least, top_value):
    factor_of, own = 1.0, jax.random.fold_in(own_key, 6)
    for position, parts in pieces:
        draws = jnp.exp(jax.random.uniform(jax.random.fold_in(own, position), (parts,), jnp.float32, least / len(pieces), top_value / len(pieces)))
        factor_of = factor_of * jnp.repeat(draws, dims[position] // parts).reshape([-1 if axis == position else 1 for axis in range(len(dims))])
    return factor_of


def gaussian(key, shape, scale, most, cuts=(), kind=jnp.bfloat16):
    loudness = block_scale(key, shape, cuts, -0.22, 0.18) if cuts else 1.0
    entries = jax.random.normal(key, shape, jnp.float32) * scale * loudness
    return jnp.minimum(jnp.maximum(entries, -most), most).astype(kind)


def setup_inputs(seed: int = 0, part: int = 0) -> dict:
    key_of = jax.random.split(jax.random.key(seed), 8)
    part_splits = jax.random.split(jax.random.fold_in(key_of[7], part), 8)
    return {
        "queries": draw_queries(jax.random.fold_in(jax.random.fold_in(key_of[7], part), 71), part),
        "keys_values": draw_keys_values(jax.random.fold_in(jax.random.fold_in(key_of[7], part), 71), part),
        "latents": gaussian(part_splits[2], (NS, SPAN_TOK, D), 1.0, 6.0, ((0, 4), (1, 4))),
        "out_weight": gaussian(key_of[3], (HQ, D), (max(HD // 32, 1)) ** -0.5, 3.0, ((0, 4),)),
        "gate_table": jnp.clip(jax.random.uniform(key_of[4], (LEVELS, D), jnp.float32, 0.5, 1.5), 0.5, 1.5),
        "level_index": with_ends(jax.random.randint(part_splits[5], (NS,), 0, LEVELS), jax.random.fold_in(part_splits[5], 1), 0, LEVELS - 1).astype(jnp.int32),
        "pair_window": draw_pair_window(jax.random.fold_in(jax.random.fold_in(key_of[7], part), 71), part),
    }


NEG_BIG = -1e+30

def reference(queries, keys_values, latents, out_weight, gate_table, level_index, pair_window):
    sections, span_tok, width_all = queries.shape
    head_count = width_all // HD
    score_scale = 1.0 / math.sqrt(HD)
    final_pair = sections - 2
    row_ids = jnp.arange(span_tok, dtype=jnp.int32)

    def one_section(section_id):
        prev_width = jnp.where(section_id > 0, pair_window[jnp.clip(section_id - 1, 0, final_pair)], 0)
        next_width = jnp.where(section_id < sections - 1, pair_window[jnp.clip(section_id, 0, final_pair)], 0)
        lower_id = jnp.clip(section_id - 1, 0, sections - 1)
        upper_id = jnp.clip(section_id + 1, 0, sections - 1)
        key_rows = jnp.concatenate([keys_values[0, lower_id], keys_values[0, section_id], keys_values[0, upper_id]], 0)
        value_rows = jnp.concatenate([keys_values[1, lower_id], keys_values[1, section_id], keys_values[1, upper_id]], 0)
        key_mask = jnp.concatenate([row_ids >= span_tok - prev_width, jnp.ones((span_tok,), bool), row_ids < next_width], 0)
        query_rows = queries[section_id]

        def one_head(head_id):
            col_start = head_id * HD
            query_head = lax.dynamic_slice_in_dim(query_rows, col_start, HD, 1)
            key_head = lax.dynamic_slice_in_dim(key_rows, col_start, HD, 1)
            value_head = lax.dynamic_slice_in_dim(value_rows, col_start, HD, 1)
            scores = jnp.dot(query_head, key_head.T, preferred_element_type=jnp.float32) * score_scale
            scores = jnp.where(key_mask[None, :], scores, NEG_BIG)
            row_max = lax.optimization_barrier(jnp.max(scores, axis=1, keepdims=True))
            probabilities = jnp.where(key_mask[None, :], jnp.exp(scores - row_max), 0.0)
            row_total = lax.optimization_barrier(jnp.sum(probabilities, axis=1, keepdims=True))
            weighted = jnp.dot(probabilities.astype(jnp.bfloat16), value_head, preferred_element_type=jnp.float32)
            return (weighted / row_total).astype(jnp.bfloat16)
        per_head = lax.map(one_head, jnp.arange(head_count, dtype=jnp.int32))
        attended = jnp.transpose(per_head, (1, 0, 2)).reshape(span_tok, width_all)
        projected = jnp.dot(attended, out_weight, preferred_element_type=jnp.float32)
        gate_row = gate_table[level_index[section_id]]
        return (latents[section_id].astype(jnp.float32) + gate_row[None, :] * projected).astype(jnp.bfloat16)
    updated = lax.map(one_section, jnp.arange(sections, dtype=jnp.int32))
    return jnp.roll(updated, 1, axis=0)
```

```python
import functools
import math

import jax
import jax.numpy as jnp
from jax import lax
from jax.experimental import pallas as pl
from jax.experimental.pallas import tpu as pltpu
from jax.sharding import PartitionSpec as P

HD = 128
CHUNKS = 4
NEG_BIG = -1e30
VMEM_LIMIT = 48 * 1024 * 1024


def attention_kernel(spans, cores, places, q_ref, own_ref, prev_ref, next_ref, out_ref, v_ext):
    span_tok, width = q_ref.shape
    rows = span_tok // (spans * cores)
    span_id, core_id, prev_width, next_width = (places[0], places[1], places[2], places[3])
    factor = math.log2(math.e) / math.sqrt(HD)
    col = lax.broadcasted_iota(jnp.int32, (1, span_tok), 1)
    prev_mask = col >= span_tok - prev_width
    next_mask = col < next_width
    v_ext[:, HD:] = jnp.ones((3 * span_tok, HD), v_ext.dtype)
    starts = []
    for l in range(cores - 1, -1, -1):
        for k in range(spans - 1, -1, -1):
            block = lax.rem(span_id + k, spans) * cores + lax.rem(core_id + l, cores)
            starts.append(pl.multiple_of(block * rows, rows))
    contract = (((1,), (1,)), ((), ()))
    for h in range(width // HD):
        head = slice(h * HD, (h + 1) * HD)
        q = jnp.concatenate([q_ref[pl.ds(s, rows), head] for s in starts], axis=0)
        s_prev = lax.dot_general(q, prev_ref[0, :, head], contract, preferred_element_type=jnp.float32)
        s_own = lax.dot_general(q, own_ref[0, :, head], contract, preferred_element_type=jnp.float32)
        s_next = lax.dot_general(q, next_ref[0, :, head], contract, preferred_element_type=jnp.float32)
        s_prev = jnp.where(prev_mask, s_prev, NEG_BIG)
        s_next = jnp.where(next_mask, s_next, NEG_BIG)
        scores = jnp.concatenate([s_prev, s_own, s_next], axis=1)
        top = jnp.max(scores, axis=1, keepdims=True)
        probs = jnp.exp2((scores - top) * factor).astype(jnp.bfloat16)
        v_ext[:span_tok, :HD] = prev_ref[1, :, head]
        v_ext[span_tok : 2 * span_tok, :HD] = own_ref[1, :, head]
        v_ext[2 * span_tok :, :HD] = next_ref[1, :, head]
        both = jnp.dot(probs, v_ext[...], preferred_element_type=jnp.float32)
        out_ref[:, head] = (both[:, :HD] / both[:, HD:]).astype(out_ref.dtype)


def attention(spans, cores, places, queries, own, before, after):
    span_tok, width = queries.shape
    whole = pl.BlockSpec(memory_space=pltpu.VMEM)
    return pl.pallas_call(
        functools.partial(attention_kernel, spans, cores),
        out_shape=jax.ShapeDtypeStruct((span_tok, width), jnp.bfloat16),
        in_specs=[pl.BlockSpec(memory_space=pltpu.SMEM)] + [whole] * 4,
        out_specs=whole,
        scratch_shapes=[pltpu.VMEM((3 * span_tok, 2 * HD), jnp.bfloat16)],
        compiler_params=pltpu.CompilerParams(vmem_limit_bytes=VMEM_LIMIT),
        cost_estimate=pl.CostEstimate(
            flops=12 * span_tok * span_tok * width,
            bytes_accessed=16 * span_tok * width,
            transcendentals=3 * span_tok * span_tok * width // HD,
        ),
        name="attention",
    )(places, queries, own, before, after)


def project_kernel(parts, rows, *refs):
    att, weights, (send_ref, keep_ref) = refs[:parts], refs[parts : 2 * parts], refs[2 * parts :]
    total = jnp.dot(att[0][...], weights[0][...], preferred_element_type=jnp.float32)
    for a, w in zip(att[1:], weights[1:]):
        total += jnp.dot(a[...], w[...], preferred_element_type=jnp.float32)
    send_ref[...] = total[:-rows].astype(send_ref.dtype)
    keep_ref[...] = total[-rows:]


def project(att, weights, rows, chunk, chunks):
    parts = len(att)
    all_rows, depth = att[0].shape
    columns = weights[0].shape[1] // chunks
    tile = columns
    for size in (640, 512, 256, 128):
        if columns % size == 0:
            tile = size
            break
    steps = columns // tile
    first = chunk * steps
    return pl.pallas_call(
        functools.partial(project_kernel, parts, rows),
        grid=(steps,),
        out_shape=(
            jax.ShapeDtypeStruct((all_rows - rows, columns), jnp.bfloat16),
            jax.ShapeDtypeStruct((rows, columns), jnp.float32),
        ),
        in_specs=[pl.BlockSpec((all_rows, depth), lambda t: (0, 0))] * parts
        + [pl.BlockSpec((depth, tile), lambda t: (0, first + t))] * parts,
        out_specs=(
            pl.BlockSpec((all_rows - rows, tile), lambda t: (0, t)),
            pl.BlockSpec((rows, tile), lambda t: (0, t)),
        ),
        compiler_params=pltpu.CompilerParams(vmem_limit_bytes=VMEM_LIMIT),
        cost_estimate=pl.CostEstimate(
            flops=2 * parts * all_rows * depth * columns,
            bytes_accessed=2 * parts * depth * columns,
            transcendentals=0,
        ),
        name="project",
    )(*att, *weights)


def rotate(value, axis, steps):
    count = lax.axis_size(axis)
    return lax.ppermute(value, axis, [(i, (i + steps) % count) for i in range(count)])


def shards(queries, keys_values, latents, out_weight, gate_table, level_index, pair_window):
    sections, spans, cores = (lax.axis_size(a) for a in ("section", "span", "mp"))
    section_id = lax.axis_index("section")
    rows = latents.shape[1]
    final_pair = pair_window.shape[0] - 1
    prev_width = jnp.where(section_id > 0, pair_window[jnp.clip(section_id - 1, 0, final_pair)], 0)
    next_width = jnp.where(
        section_id < sections - 1, pair_window[jnp.clip(section_id, 0, final_pair)], 0
    )
    places = jnp.stack(
        [lax.axis_index("span"), lax.axis_index("mp"), prev_width, next_width]
    ).astype(jnp.int32)
    up = [(i, i + 1) for i in range(sections - 1)]
    down = [(j, i) for i, j in up]
    before = lax.ppermute(keys_values, "section", up)
    after = lax.ppermute(keys_values, "section", down)
    weights = [out_weight] + [rotate(out_weight, "mp", l) for l in range(1, cores)]
    gate_row = gate_table[level_index[0]]

    attended = attention(
        spans, cores, places, queries[0], keys_values[:, 0], before[:, 0], after[:, 0]
    )
    per_core = spans * rows
    att = [attended[(cores - 1) * per_core :]]
    for l in range(1, cores):
        att.append(rotate(attended[(cores - 1 - l) * per_core : (cores - l) * per_core], "mp", l))

    columns = latents.shape[2] // CHUNKS
    pieces = []
    for c in range(CHUNKS):
        send, keep = project(att, weights, rows, c, CHUNKS)
        total = keep
        for k in range(1, spans):
            block = send[(spans - 1 - k) * rows : (spans - k) * rows]
            total = total + rotate(block, "span", k).astype(jnp.float32)
        part = slice(c * columns, (c + 1) * columns)
        updated = latents[0, :, part].astype(jnp.float32) + gate_row[None, part] * total
        pieces.append(rotate(updated.astype(jnp.bfloat16), "section", 1))
    return jnp.concatenate(pieces, axis=1)[None]


def solution(mesh):
    in_specs = (
        P(("group", "section"), None, ("span", "mp")),
        P(None, ("group", "section"), None, ("span", "mp")),
        P(("group", "section"), ("span", "mp"), None),
        P(("span", "mp"), None),
        P(),
        P(("group", "section")),
        P("group"),
    )
    out_specs = P(("group", "section"), ("span", "mp"), None)
    return jax.shard_map(shards, mesh=mesh, in_specs=in_specs, out_specs=out_specs, check_vma=False)
```

```python
import functools
import math

import jax
import jax.numpy as jnp
from jax import lax
from jax.experimental import pallas as pl
from jax.experimental.pallas import tpu as pltpu
from jax.sharding import PartitionSpec as P

HD = 128
CHUNKS = 4
NEG_BIG = -1e30
VMEM_LIMIT = 12 * 1024 * 1024


def send_order(spans, cores, rows, span_id, core_id):
    groups = []
    for l in range(cores - 1, -1, -1):
        starts = []
        for k in range(spans - 1, -1, -1):
            block = lax.rem(span_id + k, spans) * cores + lax.rem(core_id + l, cores)
            starts.append(pl.multiple_of(block * rows, rows))
        groups.append(starts)
    return groups


def scores_of(q, keys):
    return lax.dot_general(
        q, keys, (((1,), (1,)), ((), ())), preferred_element_type=jnp.float32
    )


def first_kernel(
    spans, cores, places, q_ref, own_ref, prev_ref, acc_ref, den_ref, top_ref, v_ext
):
    span_tok, width = q_ref.shape
    rows = span_tok // (spans * cores)
    factor = math.log2(math.e) / math.sqrt(HD)
    col = lax.broadcasted_iota(jnp.int32, (1, span_tok), 1)
    prev_mask = col >= span_tok - places[2]
    v_ext[:, HD:] = jnp.ones((2 * span_tok, HD), v_ext.dtype)
    starts = sum(send_order(spans, cores, rows, places[0], places[1]), [])
    for h in range(width // HD):
        head = slice(h * HD, (h + 1) * HD)
        q = jnp.concatenate([q_ref[pl.ds(s, rows), head] for s in starts], axis=0)
        s_prev = jnp.where(prev_mask, scores_of(q, prev_ref[0, 0, :, head]), NEG_BIG)
        s_own = scores_of(q, own_ref[0, 0, :, head])
        scores = jnp.concatenate([s_prev, s_own], axis=1)
        top = jnp.max(scores, axis=1, keepdims=True)
        probs = jnp.exp2((scores - top) * factor).astype(jnp.bfloat16)
        v_ext[:span_tok, :HD] = prev_ref[1, 0, :, head]
        v_ext[span_tok:, :HD] = own_ref[1, 0, :, head]
        both = jnp.dot(probs, v_ext[...], preferred_element_type=jnp.float32)
        acc_ref[:, head] = both[:, :HD]
        den_ref[:, head] = both[:, HD:]
        top_ref[:, head] = jnp.broadcast_to(top, (span_tok, HD))


def second_kernel(
    spans, cores, l, places, q_ref, next_ref, acc_ref, den_ref, top_ref, out_ref, v_ext
):
    span_tok, width = q_ref.shape
    rows = span_tok // (spans * cores)
    factor = math.log2(math.e) / math.sqrt(HD)
    col = lax.broadcasted_iota(jnp.int32, (1, span_tok), 1)
    next_mask = col < places[3]
    v_ext[:, HD:] = jnp.ones((span_tok, HD), v_ext.dtype)
    starts = send_order(spans, cores, rows, places[0], places[1])[cores - 1 - l]
    part = slice((cores - 1 - l) * spans * rows, (cores - l) * spans * rows)
    for h in range(width // HD):
        head = slice(h * HD, (h + 1) * HD)
        q = jnp.concatenate([q_ref[pl.ds(s, rows), head] for s in starts], axis=0)
        scores = jnp.where(next_mask, scores_of(q, next_ref[0, 0, :, head]), NEG_BIG)
        before = top_ref[part, head]
        top = jnp.maximum(before, jnp.max(scores, axis=1, keepdims=True))
        probs = jnp.exp2((scores - top[:, :1]) * factor).astype(jnp.bfloat16)
        fade = jnp.exp2((before - top) * factor)
        v_ext[:, :HD] = next_ref[1, 0, :, head]
        both = jnp.dot(probs, v_ext[...], preferred_element_type=jnp.float32)
        weighted = acc_ref[part, head] * fade + both[:, :HD]
        total = den_ref[part, head] * fade + both[:, HD:]
        out_ref[:, head] = (weighted / total).astype(out_ref.dtype)


SMEM_SPEC = pl.BlockSpec(memory_space=pltpu.SMEM)
VMEM_SPEC = pl.BlockSpec(memory_space=pltpu.VMEM)


def attend_first(spans, cores, places, queries, own, before):
    span_tok, width = queries.shape
    state = jax.ShapeDtypeStruct((span_tok, width), jnp.float32)
    return pl.pallas_call(
        functools.partial(first_kernel, spans, cores),
        out_shape=(state,) * 3,
        in_specs=[SMEM_SPEC] + [VMEM_SPEC] * 3,
        out_specs=(VMEM_SPEC,) * 3,
        scratch_shapes=[pltpu.VMEM((2 * span_tok, 2 * HD), jnp.bfloat16)],
        compiler_params=pltpu.CompilerParams(vmem_limit_bytes=VMEM_LIMIT),
        cost_estimate=pl.CostEstimate(
            flops=8 * span_tok * span_tok * width,
            bytes_accessed=22 * span_tok * width,
            transcendentals=2 * span_tok * span_tok * width // HD,
        ),
        name="attend_first",
    )(places, queries, own, before)


def attend_second(spans, cores, l, places, queries, after, state):
    span_tok, width = queries.shape
    return pl.pallas_call(
        functools.partial(second_kernel, spans, cores, l),
        out_shape=jax.ShapeDtypeStruct((span_tok // cores, width), jnp.bfloat16),
        in_specs=[SMEM_SPEC] + [VMEM_SPEC] * 5,
        out_specs=VMEM_SPEC,
        scratch_shapes=[pltpu.VMEM((span_tok, 2 * HD), jnp.bfloat16)],
        compiler_params=pltpu.CompilerParams(vmem_limit_bytes=VMEM_LIMIT),
        cost_estimate=pl.CostEstimate(
            flops=4 * span_tok * span_tok * width // cores,
            bytes_accessed=10 * span_tok * width,
            transcendentals=span_tok * span_tok * width // HD // cores,
        ),
        name="attend_second",
    )(places, queries, after, *state)


def project_kernel(parts, rows, first, *refs):
    att, weights, outs = refs[:parts], refs[parts : 2 * parts], refs[2 * parts :]
    columns = outs[-1].shape[1]
    tile = math.gcd(columns, 256)
    for t in range(0, columns, tile):
        total = None
        for a, w in zip(att, weights):
            term = jnp.dot(
                a[...], w[:, first + t : first + t + tile], preferred_element_type=jnp.float32
            )
            total = term if total is None else total + term
        for i, out in enumerate(outs):
            out[:, t : t + tile] = total[i * rows : (i + 1) * rows].astype(out.dtype)


def project(att, weights, rows, first, columns):
    parts = len(att)
    all_rows, depth = att[0].shape
    send = jax.ShapeDtypeStruct((rows, columns), jnp.bfloat16)
    keep = jax.ShapeDtypeStruct((rows, columns), jnp.float32)
    blocks = all_rows // rows
    return pl.pallas_call(
        functools.partial(project_kernel, parts, rows, first),
        out_shape=(send,) * (blocks - 1) + (keep,),
        in_specs=[VMEM_SPEC] * (2 * parts),
        out_specs=(VMEM_SPEC,) * blocks,
        compiler_params=pltpu.CompilerParams(vmem_limit_bytes=VMEM_LIMIT),
        cost_estimate=pl.CostEstimate(
            flops=2 * parts * all_rows * depth * columns,
            bytes_accessed=2 * parts * depth * columns,
            transcendentals=0,
        ),
        name="project",
    )(*att, *weights)


def combine_kernel(first, level, latents_ref, gate_ref, keep_ref, *refs):
    others, out_ref = refs[:-1], refs[-1]
    part = slice(first, first + keep_ref.shape[1])
    total = keep_ref[...]
    for other in others:
        total += other[...].astype(jnp.float32)
    gate = gate_ref[pl.ds(level[0], 1), part]
    out_ref[...] = (latents_ref[:, part].astype(jnp.float32) + gate * total).astype(out_ref.dtype)


def combine(level, latents, gates, keep, others, first):
    rows, columns = keep.shape
    return pl.pallas_call(
        functools.partial(combine_kernel, first),
        out_shape=jax.ShapeDtypeStruct((rows, columns), latents.dtype),
        in_specs=[SMEM_SPEC] + [VMEM_SPEC] * (3 + len(others)),
        out_specs=VMEM_SPEC,
        compiler_params=pltpu.CompilerParams(vmem_limit_bytes=VMEM_LIMIT),
        cost_estimate=pl.CostEstimate(
            flops=4 * rows * columns, bytes_accessed=12 * rows * columns, transcendentals=0
        ),
        name="combine",
    )(level, latents, gates, keep, *others)


def rotate(value, axis, steps):
    count = lax.axis_size(axis)
    return lax.ppermute(value, axis, [(i, (i + steps) % count) for i in range(count)])


def shards(queries, keys_values, latents, out_weight, gate_table, level_index, pair_window):
    sections, spans, cores = (lax.axis_size(a) for a in ("section", "span", "mp"))
    section_id = lax.axis_index("section")
    rows = latents.shape[1]
    final_pair = pair_window.shape[0] - 1
    prev_width = jnp.where(section_id > 0, pair_window[jnp.clip(section_id - 1, 0, final_pair)], 0)
    next_width = jnp.where(
        section_id < sections - 1, pair_window[jnp.clip(section_id, 0, final_pair)], 0
    )
    places = jnp.stack(
        [lax.axis_index("span"), lax.axis_index("mp"), prev_width, next_width]
    ).astype(jnp.int32)
    up = [(i, i + 1) for i in range(sections - 1)]
    down = [(j, i) for i, j in up]
    before = lax.ppermute(keys_values, "section", up)
    after = lax.ppermute(keys_values, "section", down)
    weights = [out_weight] + [rotate(out_weight, "mp", l) for l in range(1, cores)]
    own_queries, own_latents = queries[0], latents[0]
    state = attend_first(spans, cores, places, own_queries, keys_values, before)
    att = []
    for l in range(cores - 1, -1, -1):
        out = attend_second(spans, cores, l, places, own_queries, after, state)
        att.insert(0, out if l == 0 else rotate(out, "mp", l))

    columns = latents.shape[2] // CHUNKS
    pieces = []
    for first in range(0, latents.shape[2], columns):
        *send, keep = project(att, weights, rows, first, columns)
        others = [rotate(send[spans - 1 - k], "span", k) for k in range(1, spans)]
        updated = combine(level_index, own_latents, gate_table, keep, others, first)
        pieces.append(rotate(updated, "section", 1))
    return jnp.concatenate(pieces, axis=1)[None]


def solution(mesh):
    in_specs = (
        P(("group", "section"), None, ("span", "mp")),
        P(None, ("group", "section"), None, ("span", "mp")),
        P(("group", "section"), ("span", "mp"), None),
        P(("span", "mp"), None),
        P(),
        P(("group", "section")),
        P("group"),
    )
    out_specs = P(("group", "section"), ("span", "mp"), None)
    return jax.shard_map(shards, mesh=mesh, in_specs=in_specs, out_specs=out_specs, check_vma=False)
```

```python
import functools
import math

import jax
import jax.numpy as jnp
from jax import lax
from jax.experimental import pallas as pl
from jax.experimental.pallas import tpu as pltpu
from jax.sharding import PartitionSpec as P

HD = 128
CHUNKS = 4
NEG_BIG = -1e30
VMEM_LIMIT = 4 * 1024 * 1024


def scores_of(q, keys):
    return lax.dot_general(
        q, keys, (((1,), (1,)), ((), ())), preferred_element_type=jnp.float32
    )


FACTOR = math.log2(math.e) / math.sqrt(HD)


def own_kernel(q_ref, own_ref, acc_ref, den_ref, top_ref):
    rows, width = q_ref.shape
    ones = jnp.ones((own_ref.shape[2], HD), jnp.bfloat16)
    for h in range(width // HD):
        head = slice(h * HD, (h + 1) * HD)
        scores = scores_of(q_ref[:, head], own_ref[0, 0, :, head])
        top = jnp.max(scores, axis=1, keepdims=True)
        probs = jnp.exp2((scores - top) * FACTOR).astype(jnp.bfloat16)
        values = jnp.concatenate([own_ref[1, 0, :, head], ones], axis=1)
        both = jnp.dot(probs, values, preferred_element_type=jnp.float32)
        acc_ref[:, head] = both[:, :HD]
        den_ref[:, head] = both[:, HD:]
        top_ref[:, head] = jnp.broadcast_to(top, (rows, HD))


def halo_kernel(
    first, last, q_ref, halo_ref, mask_ref, acc_ref, den_ref, top_ref, *outs
):
    rows, width = outs[0].shape
    part = slice(first, first + rows)
    mask = mask_ref[...]
    ones = jnp.ones((halo_ref.shape[2], HD), jnp.bfloat16)
    for h in range(width // HD):
        head = slice(h * HD, (h + 1) * HD)
        scores = scores_of(q_ref[part, head], halo_ref[0, 0, :, head]) + mask
        before = top_ref[part, head]
        top = jnp.maximum(before, jnp.max(scores, axis=1, keepdims=True))
        probs = jnp.exp2((scores - top[:, :1]) * FACTOR).astype(jnp.bfloat16)
        fade = jnp.exp2((before - top) * FACTOR)
        values = jnp.concatenate([halo_ref[1, 0, :, head], ones], axis=1)
        both = jnp.dot(probs, values, preferred_element_type=jnp.float32)
        weighted = acc_ref[part, head] * fade + both[:, :HD]
        total = den_ref[part, head] * fade + both[:, HD:]
        if last:
            outs[0][:, head] = (weighted / total).astype(outs[0].dtype)
        else:
            outs[0][:, head] = weighted
            outs[1][:, head] = total
            outs[2][:, head] = top


SMEM_SPEC = pl.BlockSpec(memory_space=pltpu.SMEM)
VMEM_SPEC = pl.BlockSpec(memory_space=pltpu.VMEM)


def attend_own(queries, own):
    rows, width = queries.shape
    span_tok = own.shape[2]
    state = jax.ShapeDtypeStruct((rows, width), jnp.float32)
    return pl.pallas_call(
        own_kernel,
        out_shape=(state,) * 3,
        in_specs=[VMEM_SPEC] * 2,
        out_specs=(VMEM_SPEC,) * 3,
        compiler_params=pltpu.CompilerParams(vmem_limit_bytes=VMEM_LIMIT),
        cost_estimate=pl.CostEstimate(
            flops=4 * rows * span_tok * width,
            bytes_accessed=18 * span_tok * width,
            transcendentals=rows * span_tok * width // HD,
        ),
        name="attend_own",
    )(queries, own)


def attend_halo(queries, halo, mask, state, first, rows, last):
    width = queries.shape[1]
    span_tok = halo.shape[2]
    if last:
        out_shape = (jax.ShapeDtypeStruct((rows, width), jnp.bfloat16),)
    else:
        out_shape = (jax.ShapeDtypeStruct((rows, width), jnp.float32),) * 3
    return pl.pallas_call(
        functools.partial(halo_kernel, first, last),
        out_shape=out_shape,
        in_specs=[VMEM_SPEC] * 6,
        out_specs=(VMEM_SPEC,) * len(out_shape),
        compiler_params=pltpu.CompilerParams(vmem_limit_bytes=VMEM_LIMIT),
        cost_estimate=pl.CostEstimate(
            flops=4 * rows * span_tok * width,
            bytes_accessed=20 * rows * width,
            transcendentals=rows * span_tok * width // HD,
        ),
        name="attend_halo",
    )(queries, halo, mask, *state)


def hold_kernel(src_ref, dst_ref, sem):
    copy = pltpu.make_async_copy(src_ref, dst_ref, sem)
    copy.start()
    copy.wait()


def hold(array):
    return pl.pallas_call(
        hold_kernel,
        out_shape=jax.ShapeDtypeStruct(array.shape, array.dtype),
        in_specs=[pl.BlockSpec(memory_space=pl.ANY)],
        out_specs=VMEM_SPEC,
        scratch_shapes=[pltpu.SemaphoreType.DMA],
        compiler_params=pltpu.CompilerParams(vmem_limit_bytes=VMEM_LIMIT),
        cost_estimate=pl.CostEstimate(flops=0, bytes_accessed=2 * array.size * 2, transcendentals=0),
        name="hold",
    )(array)


def project_kernel(parts, rows, first, *refs):
    att, weights, outs = refs[:parts], refs[parts : 2 * parts], refs[2 * parts :]
    columns = outs[-1].shape[1]
    tile = math.gcd(columns, 256)
    for t in range(0, columns, tile):
        total = None
        for a, w in zip(att, weights):
            term = jnp.dot(
                a[...], w[:, first + t : first + t + tile], preferred_element_type=jnp.float32
            )
            total = term if total is None else total + term
        for i, out in enumerate(outs):
            out[:, t : t + tile] = total[i * rows : (i + 1) * rows].astype(out.dtype)


def project(att, weights, rows, first, columns):
    parts = len(att)
    all_rows, depth = att[0].shape
    send = jax.ShapeDtypeStruct((rows, columns), jnp.bfloat16)
    keep = jax.ShapeDtypeStruct((rows, columns), jnp.float32)
    blocks = all_rows // rows
    return pl.pallas_call(
        functools.partial(project_kernel, parts, rows, first),
        out_shape=(send,) * (blocks - 1) + (keep,),
        in_specs=[VMEM_SPEC] * (2 * parts),
        out_specs=(VMEM_SPEC,) * blocks,
        compiler_params=pltpu.CompilerParams(vmem_limit_bytes=VMEM_LIMIT),
        cost_estimate=pl.CostEstimate(
            flops=2 * parts * all_rows * depth * columns,
            bytes_accessed=2 * parts * depth * columns,
            transcendentals=0,
        ),
        name="project",
    )(*att, *weights)


def combine_kernel(first, level, latents_ref, gate_ref, keep_ref, *refs):
    others, out_ref = refs[:-1], refs[-1]
    part = slice(first, first + keep_ref.shape[1])
    total = keep_ref[...]
    for other in others:
        total += other[...].astype(jnp.float32)
    gate = gate_ref[pl.ds(level[0], 1), part]
    out_ref[...] = (latents_ref[:, part].astype(jnp.float32) + gate * total).astype(out_ref.dtype)


def combine(level, latents, gates, keep, others, first):
    rows, columns = keep.shape
    return pl.pallas_call(
        functools.partial(combine_kernel, first),
        out_shape=jax.ShapeDtypeStruct((rows, columns), latents.dtype),
        in_specs=[SMEM_SPEC] + [VMEM_SPEC] * (3 + len(others)),
        out_specs=VMEM_SPEC,
        compiler_params=pltpu.CompilerParams(vmem_limit_bytes=VMEM_LIMIT),
        cost_estimate=pl.CostEstimate(
            flops=4 * rows * columns, bytes_accessed=12 * rows * columns, transcendentals=0
        ),
        name="combine",
    )(level, latents, gates, keep, *others)


def rotate(value, axis, steps):
    count = lax.axis_size(axis)
    return lax.ppermute(value, axis, [(i, (i + steps) % count) for i in range(count)])


def shards(queries, keys_values, latents, out_weight, gate_table, level_index, pair_window):
    sections, spans, cores = (lax.axis_size(a) for a in ("section", "span", "mp"))
    section_id = lax.axis_index("section")
    rows = latents.shape[1]
    final_pair = pair_window.shape[0] - 1
    prev_width = jnp.where(section_id > 0, pair_window[jnp.clip(section_id - 1, 0, final_pair)], 0)
    next_width = jnp.where(
        section_id < sections - 1, pair_window[jnp.clip(section_id, 0, final_pair)], 0
    )
    up = [(i, i + 1) for i in range(sections - 1)]
    down = [(j, i) for i, j in up]
    before = lax.ppermute(keys_values, "section", up)
    after = lax.ppermute(keys_values, "section", down)
    weights = [hold(out_weight)]
    weights += [hold(rotate(out_weight, "mp", l)) for l in range(1, cores)]
    own_latents = latents[0]
    span_tok = queries.shape[1]
    span_id, core_id = lax.axis_index("span"), lax.axis_index("mp")
    blocks = queries[0].reshape(spans * cores, rows, -1)
    order = []
    for l in range(cores - 1, -1, -1):
        for k in range(spans - 1, -1, -1):
            block = (span_id + k) % spans * cores + (core_id + l) % cores
            order.append(lax.dynamic_index_in_dim(blocks, block, keepdims=False))
    own_queries = jnp.concatenate(order, axis=0)
    col = jnp.arange(span_tok, dtype=jnp.int32)[None]
    prev_mask = jnp.where(col >= span_tok - prev_width, 0.0, NEG_BIG).astype(jnp.float32)
    next_mask = jnp.where(col < next_width, 0.0, NEG_BIG).astype(jnp.float32)

    state = attend_own(own_queries, keys_values)
    state, weights = lax.optimization_barrier((state, weights))
    state = attend_halo(own_queries, before, prev_mask, state, 0, span_tok, False)
    per_core = spans * rows
    att = []
    for l in range(cores - 1, -1, -1):
        start = (cores - 1 - l) * per_core
        (out,) = attend_halo(own_queries, after, next_mask, state, start, per_core, True)
        att.insert(0, out if l == 0 else rotate(out, "mp", l))

    columns = latents.shape[2] // CHUNKS
    pieces = []
    for first in range(0, latents.shape[2], columns):
        *send, keep = project(att, weights, rows, first, columns)
        others = [rotate(send[spans - 1 - k], "span", k) for k in range(1, spans)]
        updated = combine(level_index, own_latents, gate_table, keep, others, first)
        pieces.append(rotate(updated, "section", 1))
    return jnp.concatenate(pieces, axis=1)[None]


def solution(mesh):
    in_specs = (
        P(("group", "section"), None, ("span", "mp")),
        P(None, ("group", "section"), None, ("span", "mp")),
        P(("group", "section"), ("span", "mp"), None),
        P(("span", "mp"), None),
        P(),
        P(("group", "section")),
        P("group"),
    )
    out_specs = P(("group", "section"), ("span", "mp"), None)
    return jax.shard_map(shards, mesh=mesh, in_specs=in_specs, out_specs=out_specs, check_vma=False)
```

```python
import functools
import math

import jax
import jax.numpy as jnp
from jax import lax
from jax.experimental import pallas as pl
from jax.experimental.pallas import tpu as pltpu
from jax.sharding import PartitionSpec as P

HD = 128
CHUNKS = 4
NEG_BIG = -1e30
VMEM_LIMIT = 4 * 1024 * 1024


def scores_of(q, keys):
    return lax.dot_general(
        q, keys, (((1,), (1,)), ((), ())), preferred_element_type=jnp.float32
    )


FACTOR = math.log2(math.e) / math.sqrt(HD)


def exponentials(scores, top):
    wide = jnp.concatenate([top] * (scores.shape[1] // HD), axis=1)
    return jnp.exp2((scores - wide) * FACTOR).astype(jnp.bfloat16)


def own_kernel(q_ref, own_ref, acc_ref, den_ref, top_ref):
    rows, width = q_ref.shape
    ones = jnp.ones((own_ref.shape[2], HD), jnp.bfloat16)
    for h in range(width // HD):
        head = slice(h * HD, (h + 1) * HD)
        scores = scores_of(q_ref[:, head], own_ref[0, 0, :, head])
        top = jnp.broadcast_to(jnp.max(scores, axis=1, keepdims=True), (rows, HD))
        values = jnp.concatenate([own_ref[1, 0, :, head], ones], axis=1)
        both = jnp.dot(
            exponentials(scores, top), values, preferred_element_type=jnp.float32
        )
        acc_ref[:, head] = both[:, :HD]
        den_ref[:, head] = both[:, HD:]
        top_ref[:, head] = top


def halo_kernel(
    first, last, q_ref, halo_ref, mask_ref, acc_ref, den_ref, top_ref, *outs
):
    rows, width = outs[0].shape
    part = slice(first, first + rows)
    mask = mask_ref[...]
    ones = jnp.ones((halo_ref.shape[2], HD), jnp.bfloat16)
    heads = [slice(h * HD, (h + 1) * HD) for h in range(width // HD)]
    scores = [scores_of(q_ref[part, head], halo_ref[0, 0, :, head]) + mask for head in heads]
    peaks = [jnp.max(s, axis=1, keepdims=True) for s in scores]
    probs, fades = [], []
    for head, s, peak in zip(heads, scores, peaks):
        before = top_ref[part, head]
        top = jnp.maximum(before, jnp.broadcast_to(peak, before.shape))
        probs.append(exponentials(s, top))
        fades.append(jnp.exp2((before - top) * FACTOR))
        if not last:
            outs[2][:, head] = top
    for head, p, fade in zip(heads, probs, fades):
        values = jnp.concatenate([halo_ref[1, 0, :, head], ones], axis=1)
        both = jnp.dot(p, values, preferred_element_type=jnp.float32)
        weighted = acc_ref[part, head] * fade + both[:, :HD]
        total = den_ref[part, head] * fade + both[:, HD:]
        if last:
            outs[0][:, head] = (weighted / total).astype(outs[0].dtype)
        else:
            outs[0][:, head] = weighted
            outs[1][:, head] = total


VMEM_SPEC = pl.BlockSpec(memory_space=pltpu.VMEM)


def attend(kernel, name, out_shape, flops, *operands):
    return pl.pallas_call(
        kernel,
        out_shape=out_shape,
        in_specs=[VMEM_SPEC] * len(operands),
        out_specs=(VMEM_SPEC,) * len(out_shape),
        compiler_params=pltpu.CompilerParams(vmem_limit_bytes=VMEM_LIMIT),
        cost_estimate=pl.CostEstimate(
            flops=flops,
            bytes_accessed=sum(x.size * x.dtype.itemsize for x in operands),
            transcendentals=flops // (4 * HD),
        ),
        name=name,
    )(*operands)


def hold_kernel(src_ref, dst_ref, sem):
    copy = pltpu.make_async_copy(src_ref, dst_ref, sem)
    copy.start()
    copy.wait()


def hold(array):
    return pl.pallas_call(
        hold_kernel,
        out_shape=jax.ShapeDtypeStruct(array.shape, array.dtype),
        in_specs=[pl.BlockSpec(memory_space=pltpu.HBM)],
        out_specs=VMEM_SPEC,
        scratch_shapes=[pltpu.SemaphoreType.DMA],
        compiler_params=pltpu.CompilerParams(vmem_limit_bytes=VMEM_LIMIT),
        cost_estimate=pl.CostEstimate(flops=0, bytes_accessed=1024, transcendentals=0),
        name="hold",
    )(array)


def project_kernel(parts, rows, first, base, *refs):
    att, weights = refs[:parts], refs[parts : 2 * parts]
    outs = refs[2 * parts + (1 if base else 0) :]
    columns = outs[-1].shape[1]
    tile = math.gcd(columns, 256)
    for t in range(0, columns, tile):
        total = refs[2 * parts][:, t : t + tile] if base else None
        for a, w in zip(att, weights):
            term = jnp.dot(
                a[...], w[:, first + t : first + t + tile], preferred_element_type=jnp.float32
            )
            total = term if total is None else total + term
        if len(outs) == 1:
            outs[0][:, t : t + tile] = total
            continue
        for i, out in enumerate(outs):
            out[:, t : t + tile] = total[i * rows : (i + 1) * rows].astype(out.dtype)


def project(att, weights, base, rows, first, columns, split):
    parts = len(att)
    all_rows, depth = att[0].shape
    send = jax.ShapeDtypeStruct((rows, columns), jnp.bfloat16)
    keep = jax.ShapeDtypeStruct((rows, columns), jnp.float32)
    blocks = all_rows // rows
    whole = jax.ShapeDtypeStruct((all_rows, columns), jnp.float32)
    out_shape = (send,) * (blocks - 1) + (keep,) if split else (whole,)
    bases = [] if base is None else [base]
    return pl.pallas_call(
        functools.partial(project_kernel, parts, rows, first, len(bases)),
        out_shape=out_shape,
        in_specs=[VMEM_SPEC] * (2 * parts + len(bases)),
        out_specs=(VMEM_SPEC,) * len(out_shape),
        compiler_params=pltpu.CompilerParams(vmem_limit_bytes=VMEM_LIMIT),
        cost_estimate=pl.CostEstimate(
            flops=2 * parts * all_rows * depth * columns,
            bytes_accessed=2 * parts * depth * columns,
            transcendentals=0,
        ),
        name="project",
    )(*att, *weights, *bases)


def combine_kernel(first, latents_ref, gate_ref, keep_ref, *refs):
    others, out_ref = refs[:-1], refs[-1]
    part = slice(first, first + keep_ref.shape[1])
    total = keep_ref[...]
    for other in others:
        total += other[...].astype(jnp.float32)
    out_ref[...] = (
        latents_ref[:, part].astype(jnp.float32) + gate_ref[:, part] * total
    ).astype(out_ref.dtype)


def combine(latents, gate_row, keep, others, first):
    rows, columns = keep.shape
    return pl.pallas_call(
        functools.partial(combine_kernel, first),
        out_shape=jax.ShapeDtypeStruct((rows, columns), latents.dtype),
        in_specs=[VMEM_SPEC] * (3 + len(others)),
        out_specs=VMEM_SPEC,
        compiler_params=pltpu.CompilerParams(vmem_limit_bytes=VMEM_LIMIT),
        cost_estimate=pl.CostEstimate(
            flops=4 * rows * columns, bytes_accessed=12 * rows * columns, transcendentals=0
        ),
        name="combine",
    )(latents, gate_row, keep, *others)


def rotate(value, axis, steps):
    count = lax.axis_size(axis)
    return lax.ppermute(value, axis, [(i, (i + steps) % count) for i in range(count)])


def shards(queries, keys_values, latents, out_weight, gate_table, level_index, pair_window):
    sections, spans, cores = (lax.axis_size(a) for a in ("section", "span", "mp"))
    section_id = lax.axis_index("section")
    rows = latents.shape[1]
    final_pair = pair_window.shape[0] - 1
    prev_width = jnp.where(section_id > 0, pair_window[jnp.clip(section_id - 1, 0, final_pair)], 0)
    next_width = jnp.where(
        section_id < sections - 1, pair_window[jnp.clip(section_id, 0, final_pair)], 0
    )
    up = [(i, i + 1) for i in range(sections - 1)]
    down = [(j, i) for i, j in up]
    before = lax.ppermute(keys_values, "section", up)
    after = lax.ppermute(keys_values, "section", down)
    weights = [hold(out_weight)]
    weights += [hold(rotate(out_weight, "mp", l)) for l in range(1, cores)]
    own_latents = latents[0]
    span_tok = queries.shape[1]
    span_id, core_id = lax.axis_index("span"), lax.axis_index("mp")
    blocks = queries[0].reshape(spans * cores, rows, -1)
    order = []
    for l in range(cores - 1, -1, -1):
        for k in range(spans - 1, -1, -1):
            block = (span_id + k) % spans * cores + (core_id + l) % cores
            order.append(lax.dynamic_index_in_dim(blocks, block, keepdims=False))
    own_queries = jnp.concatenate(order, axis=0)
    col = jnp.arange(span_tok, dtype=jnp.int32)[None]
    prev_mask = jnp.where(col >= span_tok - prev_width, 0.0, NEG_BIG).astype(jnp.float32)
    next_mask = jnp.where(col < next_width, 0.0, NEG_BIG).astype(jnp.float32)

    gate_row = lax.dynamic_slice_in_dim(gate_table, level_index[0], 1, axis=0)
    width = queries.shape[2]
    wide = jax.ShapeDtypeStruct((span_tok, width), jnp.float32)
    flops = 4 * span_tok * span_tok * width
    state = attend(own_kernel, "attend_own", (wide,) * 3, flops, own_queries, keys_values)
    state, weights, gate_row = lax.optimization_barrier((state, weights, gate_row))
    kernel = functools.partial(halo_kernel, 0, False)
    state = attend(
        kernel, "attend_after", (wide,) * 3, flops, own_queries, after, next_mask, *state
    )
    per_core = spans * rows
    out_shape = (jax.ShapeDtypeStruct((per_core, width), jnp.bfloat16),)
    att = []
    for l in range(cores - 1, -1, -1):
        kernel = functools.partial(halo_kernel, (cores - 1 - l) * per_core, True)
        (out,) = attend(
            kernel, "attend_before", out_shape, flops // cores,
            own_queries, before, prev_mask, *state,
        )
        att.insert(0, out if l == 0 else rotate(out, "mp", l))

    columns = latents.shape[2] // CHUNKS
    updates = []
    for c in range(CHUNKS):
        first = c * columns
        if c == 0:
            (base,) = project(att[:1], weights[:1], None, rows, first, columns, False)
            *send, keep = project(att[1:], weights[1:], base, rows, first, columns, True)
            att, keep = lax.optimization_barrier((att, keep))
        else:
            *send, keep = project(att, weights, None, rows, first, columns, True)
        others = [rotate(send[spans - 1 - k], "span", k) for k in range(1, spans)]
        updates.append(combine(own_latents, gate_row, keep, others, first))
    pieces = [rotate(update, "section", 1) for update in updates]
    early = jnp.pad(jnp.concatenate(pieces[:-1], axis=1), ((0, 0), (0, columns)))
    early, late = lax.optimization_barrier((early, pieces[-1]))
    return lax.dynamic_update_slice(early, late, (0, latents.shape[2] - columns))[None]


def solution(mesh):
    in_specs = (
        P(("group", "section"), None, ("span", "mp")),
        P(None, ("group", "section"), None, ("span", "mp")),
        P(("group", "section"), ("span", "mp"), None),
        P(("span", "mp"), None),
        P(),
        P(("group", "section")),
        P("group"),
    )
    out_specs = P(("group", "section"), ("span", "mp"), None)
    return jax.shard_map(shards, mesh=mesh, in_specs=in_specs, out_specs=out_specs, check_vma=False)
```

```python
import functools
import math

import jax
import jax.numpy as jnp
from jax import lax
from jax.experimental import pallas as pl
from jax.experimental.pallas import tpu as pltpu
from jax.sharding import PartitionSpec as P

HD = 128
CHUNKS = 4
NEG_BIG = -1e30
VMEM_LIMIT = 4 * 1024 * 1024


def scores_of(q, keys):
    return lax.dot_general(
        q, keys, (((1,), (1,)), ((), ())), preferred_element_type=jnp.float32
    )


FACTOR = math.log2(math.e) / math.sqrt(HD)


def exponentials(scores, top):
    wide = jnp.concatenate([top] * (scores.shape[1] // HD), axis=1)
    return jnp.exp2((scores - wide) * FACTOR).astype(jnp.bfloat16)


def own_kernel(q_ref, own_ref, acc_ref, den_ref, top_ref):
    rows, width = q_ref.shape
    ones = jnp.ones((own_ref.shape[2], HD), jnp.bfloat16)
    for h in range(width // HD):
        head = slice(h * HD, (h + 1) * HD)
        scores = scores_of(q_ref[:, head], own_ref[0, 0, :, head])
        top = jnp.broadcast_to(jnp.max(scores, axis=1, keepdims=True), (rows, HD))
        values = jnp.concatenate([own_ref[1, 0, :, head], ones], axis=1)
        both = jnp.dot(
            exponentials(scores, top), values, preferred_element_type=jnp.float32
        )
        acc_ref[:, head] = both[:, :HD]
        den_ref[:, head] = both[:, HD:]
        top_ref[:, head] = top


def halo_kernel(
    first, last, q_ref, halo_ref, mask_ref, acc_ref, den_ref, top_ref, *outs
):
    rows, width = outs[0].shape
    part = slice(first, first + rows)
    mask = mask_ref[...]
    ones = jnp.ones((halo_ref.shape[2], HD), jnp.bfloat16)
    heads = [slice(h * HD, (h + 1) * HD) for h in range(width // HD)]
    scores = [scores_of(q_ref[part, head], halo_ref[0, 0, :, head]) + mask for head in heads]
    peaks = [jnp.max(s, axis=1, keepdims=True) for s in scores]
    probs, fades = [], []
    for head, s, peak in zip(heads, scores, peaks):
        before = top_ref[part, head]
        top = jnp.maximum(before, jnp.broadcast_to(peak, before.shape))
        probs.append(exponentials(s, top))
        fades.append(jnp.exp2((before - top) * FACTOR))
        if not last:
            outs[2][:, head] = top
    for head, p, fade in zip(heads, probs, fades):
        values = jnp.concatenate([halo_ref[1, 0, :, head], ones], axis=1)
        both = jnp.dot(p, values, preferred_element_type=jnp.float32)
        weighted = acc_ref[part, head] * fade + both[:, :HD]
        total = den_ref[part, head] * fade + both[:, HD:]
        if last:
            outs[0][:, head] = (weighted / total).astype(outs[0].dtype)
        else:
            outs[0][:, head] = weighted
            outs[1][:, head] = total


VMEM_SPEC = pl.BlockSpec(memory_space=pltpu.VMEM)


def attend(kernel, name, out_shape, flops, *operands):
    return pl.pallas_call(
        kernel,
        out_shape=out_shape,
        in_specs=[VMEM_SPEC] * len(operands),
        out_specs=(VMEM_SPEC,) * len(out_shape),
        compiler_params=pltpu.CompilerParams(vmem_limit_bytes=VMEM_LIMIT),
        cost_estimate=pl.CostEstimate(
            flops=flops,
            bytes_accessed=sum(x.size * x.dtype.itemsize for x in operands),
            transcendentals=flops // (4 * HD),
        ),
        name=name,
    )(*operands)


def hold_kernel(src_ref, dst_ref, sem):
    copy = pltpu.make_async_copy(src_ref, dst_ref, sem)
    copy.start()
    copy.wait()


def hold(array):
    return pl.pallas_call(
        hold_kernel,
        out_shape=jax.ShapeDtypeStruct(array.shape, array.dtype),
        in_specs=[pl.BlockSpec(memory_space=pltpu.HBM)],
        out_specs=VMEM_SPEC,
        scratch_shapes=[pltpu.SemaphoreType.DMA],
        compiler_params=pltpu.CompilerParams(vmem_limit_bytes=VMEM_LIMIT),
        cost_estimate=pl.CostEstimate(flops=0, bytes_accessed=1024, transcendentals=0),
        name="hold",
    )(array)


def project_kernel(parts, rows, first, base, *refs):
    att, weights = refs[:parts], refs[parts : 2 * parts]
    outs = refs[2 * parts + (1 if base else 0) :]
    columns = outs[-1].shape[1]
    tile = math.gcd(columns, 256)
    for t in range(0, columns, tile):
        total = refs[2 * parts][:, t : t + tile] if base else None
        for a, w in zip(att, weights):
            term = jnp.dot(
                a[...], w[:, first + t : first + t + tile], preferred_element_type=jnp.float32
            )
            total = term if total is None else total + term
        if len(outs) == 1:
            outs[0][:, t : t + tile] = total
            continue
        for i, out in enumerate(outs):
            out[:, t : t + tile] = total[i * rows : (i + 1) * rows].astype(out.dtype)


def project(att, weights, base, rows, first, columns, split):
    parts = len(att)
    all_rows, depth = att[0].shape
    send = jax.ShapeDtypeStruct((rows, columns), jnp.bfloat16)
    keep = jax.ShapeDtypeStruct((rows, columns), jnp.float32)
    blocks = all_rows // rows
    whole = jax.ShapeDtypeStruct((all_rows, columns), jnp.float32)
    out_shape = (send,) * (blocks - 1) + (keep,) if split else (whole,)
    bases = [] if base is None else [base]
    return pl.pallas_call(
        functools.partial(project_kernel, parts, rows, first, len(bases)),
        out_shape=out_shape,
        in_specs=[VMEM_SPEC] * (2 * parts + len(bases)),
        out_specs=(VMEM_SPEC,) * len(out_shape),
        compiler_params=pltpu.CompilerParams(vmem_limit_bytes=VMEM_LIMIT),
        cost_estimate=pl.CostEstimate(
            flops=2 * parts * all_rows * depth * columns,
            bytes_accessed=2 * parts * depth * columns,
            transcendentals=0,
        ),
        name="project",
    )(*att, *weights, *bases)


def combine_kernel(first, latents_ref, gate_ref, keep_ref, *refs):
    others, out_ref = refs[:-1], refs[-1]
    part = slice(first, first + keep_ref.shape[1])
    total = keep_ref[...]
    for other in others:
        total += other[...].astype(jnp.float32)
    out_ref[...] = (
        latents_ref[:, part].astype(jnp.float32) + gate_ref[:, part] * total
    ).astype(out_ref.dtype)


def combine(latents, gate_row, keep, others, first):
    rows, columns = keep.shape
    return pl.pallas_call(
        functools.partial(combine_kernel, first),
        out_shape=jax.ShapeDtypeStruct((rows, columns), latents.dtype),
        in_specs=[VMEM_SPEC] * (3 + len(others)),
        out_specs=VMEM_SPEC,
        compiler_params=pltpu.CompilerParams(vmem_limit_bytes=VMEM_LIMIT),
        cost_estimate=pl.CostEstimate(
            flops=4 * rows * columns, bytes_accessed=12 * rows * columns, transcendentals=0
        ),
        name="combine",
    )(latents, gate_row, keep, *others)


def rotate(value, axis, steps):
    count = lax.axis_size(axis)
    return lax.ppermute(value, axis, [(i, (i + steps) % count) for i in range(count)])


def shards(queries, keys_values, latents, out_weight, gate_table, level_index, pair_window):
    sections, spans, cores = (lax.axis_size(a) for a in ("section", "span", "mp"))
    section_id = lax.axis_index("section")
    rows = latents.shape[1]
    final_pair = pair_window.shape[0] - 1
    prev_width = jnp.where(section_id > 0, pair_window[jnp.clip(section_id - 1, 0, final_pair)], 0)
    next_width = jnp.where(
        section_id < sections - 1, pair_window[jnp.clip(section_id, 0, final_pair)], 0
    )
    swaps = [
        [pair for i in range(odd, sections - 1, 2) for pair in ((i, i + 1), (i + 1, i))]
        for odd in (0, 1)
    ]
    first_halo, second_halo = (lax.ppermute(keys_values, "section", pairs) for pairs in swaps)
    weights = [hold(out_weight)]
    weights += [hold(rotate(out_weight, "mp", l)) for l in range(1, cores)]
    own_latents = latents[0]
    span_tok = queries.shape[1]
    span_id, core_id = lax.axis_index("span"), lax.axis_index("mp")
    blocks = queries[0].reshape(spans * cores, rows, -1)
    order = []
    for l in range(cores - 1, -1, -1):
        for k in range(spans - 1, -1, -1):
            block = (span_id + k) % spans * cores + (core_id + l) % cores
            order.append(lax.dynamic_index_in_dim(blocks, block, keepdims=False))
    own_queries = jnp.concatenate(order, axis=0)
    col = jnp.arange(span_tok, dtype=jnp.int32)[None]
    prev_keys, next_keys = col >= span_tok - prev_width, col < next_width
    from_next = section_id % 2 == 0
    first_mask = jnp.where(jnp.where(from_next, next_keys, prev_keys), 0.0, NEG_BIG)
    second_mask = jnp.where(jnp.where(from_next, prev_keys, next_keys), 0.0, NEG_BIG)

    gate_row = lax.dynamic_slice_in_dim(gate_table, level_index[0], 1, axis=0)
    width = queries.shape[2]
    wide = jax.ShapeDtypeStruct((span_tok, width), jnp.float32)
    flops = 4 * span_tok * span_tok * width
    state = attend(own_kernel, "attend_own", (wide,) * 3, flops, own_queries, keys_values)
    state, weights, gate_row = lax.optimization_barrier((state, weights, gate_row))
    kernel = functools.partial(halo_kernel, 0, False)
    state = attend(
        kernel, "attend_first", (wide,) * 3, flops, own_queries, first_halo, first_mask, *state
    )
    per_core = spans * rows
    out_shape = (jax.ShapeDtypeStruct((per_core, width), jnp.bfloat16),)
    att = []
    for l in range(cores - 1, -1, -1):
        kernel = functools.partial(halo_kernel, (cores - 1 - l) * per_core, True)
        (out,) = attend(
            kernel, "attend_second", out_shape, flops // cores,
            own_queries, second_halo, second_mask, *state,
        )
        att.insert(0, out if l == 0 else rotate(out, "mp", l))

    columns = latents.shape[2] // CHUNKS
    updates = []
    for c in range(CHUNKS):
        first = c * columns
        if c == 0:
            (base,) = project(att[:1], weights[:1], None, rows, first, columns, False)
            *send, keep = project(att[1:], weights[1:], base, rows, first, columns, True)
            att, keep = lax.optimization_barrier((att, keep))
        else:
            *send, keep = project(att, weights, None, rows, first, columns, True)
        others = [rotate(send[spans - 1 - k], "span", k) for k in range(1, spans)]
        updates.append(combine(own_latents, gate_row, keep, others, first))
    pieces = [rotate(update, "section", 1) for update in updates]
    early = jnp.pad(jnp.concatenate(pieces[:-1], axis=1), ((0, 0), (0, columns)))
    early, late = lax.optimization_barrier((early, pieces[-1]))
    return lax.dynamic_update_slice(early, late, (0, latents.shape[2] - columns))[None]


def solution(mesh):
    in_specs = (
        P(("group", "section"), None, ("span", "mp")),
        P(None, ("group", "section"), None, ("span", "mp")),
        P(("group", "section"), ("span", "mp"), None),
        P(("span", "mp"), None),
        P(),
        P(("group", "section")),
        P("group"),
    )
    out_specs = P(("group", "section"), ("span", "mp"), None)
    return jax.shard_map(shards, mesh=mesh, in_specs=in_specs, out_specs=out_specs, check_vma=False)
```

```python
import functools
import math

import jax
import jax.numpy as jnp
from jax import lax
from jax.experimental import pallas as pl
from jax.experimental.pallas import tpu as pltpu
from jax.sharding import PartitionSpec as P

HD = 128
CHUNKS = 4
NEG_BIG = -1e30
VMEM_LIMIT = 4 * 1024 * 1024


def scores_of(q, keys):
    return lax.dot_general(
        q, keys, (((1,), (1,)), ((), ())), preferred_element_type=jnp.float32
    )


FACTOR = math.log2(math.e) / math.sqrt(HD)


def exponentials(scores, top):
    wide = jnp.concatenate([top] * (scores.shape[1] // HD), axis=1)
    return jnp.exp2((scores - wide) * FACTOR).astype(jnp.bfloat16)


def own_kernel(q_ref, own_ref, acc_ref, den_ref, top_ref):
    rows, width = q_ref.shape
    ones = jnp.ones((own_ref.shape[2], HD), jnp.bfloat16)
    for h in range(width // HD):
        head = slice(h * HD, (h + 1) * HD)
        scores = scores_of(q_ref[:, head], own_ref[0, 0, :, head])
        top = jnp.broadcast_to(jnp.max(scores, axis=1, keepdims=True), (rows, HD))
        values = jnp.concatenate([own_ref[1, 0, :, head], ones], axis=1)
        both = jnp.dot(
            exponentials(scores, top), values, preferred_element_type=jnp.float32
        )
        acc_ref[:, head] = both[:, :HD]
        den_ref[:, head] = both[:, HD:]
        top_ref[:, head] = top


def halo_kernel(halos, q_first, s_first, last, *refs):
    q_ref, refs = refs[0], refs[1:]
    halo_refs, mask_refs, refs = refs[:halos], refs[halos : 2 * halos], refs[2 * halos :]
    (acc_ref, den_ref, top_ref), outs = refs[:3], refs[3:]
    rows, width = outs[0].shape
    q_part, s_part = slice(q_first, q_first + rows), slice(s_first, s_first + rows)
    heads = [slice(h * HD, (h + 1) * HD) for h in range(width // HD)]
    masks = [mask_ref[...] for mask_ref in mask_refs]

    def visit():
        ones = jnp.ones((halos * halo_refs[0].shape[2], HD), jnp.bfloat16)
        scores = []
        for head in heads:
            q = q_ref[q_part, head]
            pieces = [scores_of(q, k[0, 0, :, head]) + m for k, m in zip(halo_refs, masks)]
            scores.append(jnp.concatenate(pieces, axis=1))
        peaks = [jnp.max(s, axis=1, keepdims=True) for s in scores]
        probs, fades = [], []
        for head, s, peak in zip(heads, scores, peaks):
            before = top_ref[s_part, head]
            top = jnp.maximum(before, jnp.broadcast_to(peak, before.shape))
            probs.append(exponentials(s, top))
            fades.append(jnp.exp2((before - top) * FACTOR))
            if not last:
                outs[2][:, head] = top
        for head, p, fade in zip(heads, probs, fades):
            values = jnp.concatenate([v[1, 0, :, head] for v in halo_refs], axis=0)
            values = jnp.concatenate([values, ones], axis=1)
            both = jnp.dot(p, values, preferred_element_type=jnp.float32)
            weighted = acc_ref[s_part, head] * fade + both[:, :HD]
            total = den_ref[s_part, head] * fade + both[:, HD:]
            if last:
                outs[0][:, head] = (weighted / total).astype(outs[0].dtype)
            else:
                outs[0][:, head] = weighted
                outs[1][:, head] = total

    if not (last and halos == 1):
        visit()
        return
    anything = jnp.max(masks[0]) == 0.0
    pl.when(anything)(visit)

    @pl.when(jnp.logical_not(anything))
    def _():
        for head in heads:
            outs[0][:, head] = (acc_ref[s_part, head] / den_ref[s_part, head]).astype(
                outs[0].dtype
            )


VMEM_SPEC = pl.BlockSpec(memory_space=pltpu.VMEM)


def attend(kernel, name, out_shape, flops, *operands):
    return pl.pallas_call(
        kernel,
        out_shape=out_shape,
        in_specs=[VMEM_SPEC] * len(operands),
        out_specs=(VMEM_SPEC,) * len(out_shape),
        compiler_params=pltpu.CompilerParams(vmem_limit_bytes=VMEM_LIMIT),
        cost_estimate=pl.CostEstimate(
            flops=flops,
            bytes_accessed=sum(x.size * x.dtype.itemsize for x in operands),
            transcendentals=flops // (4 * HD),
        ),
        name=name,
    )(*operands)


def hold_kernel(src_ref, dst_ref, sem):
    copy = pltpu.make_async_copy(src_ref, dst_ref, sem)
    copy.start()
    copy.wait()


def hold(array):
    return pl.pallas_call(
        hold_kernel,
        out_shape=jax.ShapeDtypeStruct(array.shape, array.dtype),
        in_specs=[pl.BlockSpec(memory_space=pltpu.HBM)],
        out_specs=VMEM_SPEC,
        scratch_shapes=[pltpu.SemaphoreType.DMA],
        compiler_params=pltpu.CompilerParams(vmem_limit_bytes=VMEM_LIMIT),
        cost_estimate=pl.CostEstimate(flops=0, bytes_accessed=1024, transcendentals=0),
        name="hold",
    )(array)


def project_kernel(parts, rows, first, base, *refs):
    att, weights = refs[:parts], refs[parts : 2 * parts]
    outs = refs[2 * parts + (1 if base else 0) :]
    columns = outs[-1].shape[1]
    tile = math.gcd(columns, 256)
    for t in range(0, columns, tile):
        total = refs[2 * parts][:, t : t + tile] if base else None
        for a, w in zip(att, weights):
            term = jnp.dot(
                a[...], w[:, first + t : first + t + tile], preferred_element_type=jnp.float32
            )
            total = term if total is None else total + term
        if len(outs) == 1:
            outs[0][:, t : t + tile] = total
            continue
        for i, out in enumerate(outs):
            out[:, t : t + tile] = total[i * rows : (i + 1) * rows].astype(out.dtype)


def project(att, weights, base, rows, first, columns, split):
    parts = len(att)
    all_rows, depth = att[0].shape
    send = jax.ShapeDtypeStruct((rows, columns), jnp.bfloat16)
    keep = jax.ShapeDtypeStruct((rows, columns), jnp.float32)
    blocks = all_rows // rows
    whole = jax.ShapeDtypeStruct((all_rows, columns), jnp.float32)
    out_shape = (send,) * (blocks - 1) + (keep,) if split else (whole,)
    bases = [] if base is None else [base]
    return pl.pallas_call(
        functools.partial(project_kernel, parts, rows, first, len(bases)),
        out_shape=out_shape,
        in_specs=[VMEM_SPEC] * (2 * parts + len(bases)),
        out_specs=(VMEM_SPEC,) * len(out_shape),
        compiler_params=pltpu.CompilerParams(vmem_limit_bytes=VMEM_LIMIT),
        cost_estimate=pl.CostEstimate(
            flops=2 * parts * all_rows * depth * columns,
            bytes_accessed=2 * parts * depth * columns,
            transcendentals=0,
        ),
        name="project",
    )(*att, *weights, *bases)


def combine_kernel(first, latents_ref, gate_ref, keep_ref, *refs):
    others, out_ref = refs[:-1], refs[-1]
    part = slice(first, first + keep_ref.shape[1])
    total = keep_ref[...]
    for other in others:
        total += other[...].astype(jnp.float32)
    out_ref[...] = (
        latents_ref[:, part].astype(jnp.float32) + gate_ref[:, part] * total
    ).astype(out_ref.dtype)


def combine(latents, gate_row, keep, others, first):
    rows, columns = keep.shape
    return pl.pallas_call(
        functools.partial(combine_kernel, first),
        out_shape=jax.ShapeDtypeStruct((rows, columns), latents.dtype),
        in_specs=[VMEM_SPEC] * (3 + len(others)),
        out_specs=VMEM_SPEC,
        compiler_params=pltpu.CompilerParams(vmem_limit_bytes=VMEM_LIMIT),
        cost_estimate=pl.CostEstimate(
            flops=4 * rows * columns, bytes_accessed=12 * rows * columns, transcendentals=0
        ),
        name="combine",
    )(latents, gate_row, keep, *others)


def rotate(value, axis, steps):
    count = lax.axis_size(axis)
    return lax.ppermute(value, axis, [(i, (i + steps) % count) for i in range(count)])


def shards(queries, keys_values, latents, out_weight, gate_table, level_index, pair_window):
    sections, spans, cores = (lax.axis_size(a) for a in ("section", "span", "mp"))
    section_id = lax.axis_index("section")
    rows = latents.shape[1]
    final_pair = pair_window.shape[0] - 1
    prev_width = jnp.where(section_id > 0, pair_window[jnp.clip(section_id - 1, 0, final_pair)], 0)
    next_width = jnp.where(
        section_id < sections - 1, pair_window[jnp.clip(section_id, 0, final_pair)], 0
    )
    swaps = [
        [pair for i in range(odd, sections - 1, 2) for pair in ((i, i + 1), (i + 1, i))]
        for odd in (0, 1)
    ]
    first_halo, second_halo = (lax.ppermute(keys_values, "section", pairs) for pairs in swaps)
    weights = [hold(out_weight)]
    weights += [hold(rotate(out_weight, "mp", l)) for l in range(1, cores)]
    own_latents = latents[0]
    span_tok = queries.shape[1]
    span_id, core_id = lax.axis_index("span"), lax.axis_index("mp")
    blocks = queries[0].reshape(spans * cores, rows, -1)
    order = []
    for l in range(cores - 1, -1, -1):
        for k in range(spans - 1, -1, -1):
            block = (span_id + k) % spans * cores + (core_id + l) % cores
            order.append(lax.dynamic_index_in_dim(blocks, block, keepdims=False))
    own_queries = jnp.concatenate(order, axis=0)
    col = jnp.arange(span_tok, dtype=jnp.int32)[None]
    prev_keys, next_keys = col >= span_tok - prev_width, col < next_width
    from_next = section_id % 2 == 0
    first_mask = jnp.where(jnp.where(from_next, next_keys, prev_keys), 0.0, NEG_BIG)
    second_mask = jnp.where(jnp.where(from_next, prev_keys, next_keys), 0.0, NEG_BIG)

    gate_row = lax.dynamic_slice_in_dim(gate_table, level_index[0], 1, axis=0)
    width = queries.shape[2]
    wide = jax.ShapeDtypeStruct((span_tok, width), jnp.float32)
    flops = 4 * span_tok * span_tok * width
    state = attend(own_kernel, "attend_own", (wide,) * 3, flops, own_queries, keys_values)
    state, weights, gate_row = lax.optimization_barrier((state, weights, gate_row))
    per_core = spans * rows
    some = jax.ShapeDtypeStruct((per_core, width), jnp.float32)
    out_shape = (jax.ShapeDtypeStruct((per_core, width), jnp.bfloat16),)
    att = []
    for l in range(cores - 1, 0, -1):
        start = (cores - 1 - l) * per_core
        kernel = functools.partial(halo_kernel, 1, start, start, False)
        part = attend(
            kernel, "attend_first", (some,) * 3, flops // cores,
            own_queries, first_halo, first_mask, *state,
        )
        kernel = functools.partial(halo_kernel, 1, start, 0, True)
        (out,) = attend(
            kernel, "attend_second", out_shape, flops // cores,
            own_queries, second_halo, second_mask, *part,
        )
        att.insert(0, rotate(out, "mp", l))
    start = (cores - 1) * per_core
    kernel = functools.partial(halo_kernel, 2, start, start, True)
    (out,) = attend(
        kernel, "attend_both", out_shape, 2 * flops // cores,
        own_queries, first_halo, second_halo, first_mask, second_mask, *state,
    )
    att.insert(0, out)

    columns = latents.shape[2] // CHUNKS
    updates = []
    for c in range(CHUNKS):
        first = c * columns
        if c == 0:
            (base,) = project(att[:1], weights[:1], None, rows, first, columns, False)
            *send, keep = project(att[1:], weights[1:], base, rows, first, columns, True)
            att, keep = lax.optimization_barrier((att, keep))
        else:
            *send, keep = project(att, weights, None, rows, first, columns, True)
        others = [rotate(send[spans - 1 - k], "span", k) for k in range(1, spans)]
        updates.append(combine(own_latents, gate_row, keep, others, first))
    pieces = [rotate(update, "section", 1) for update in updates]
    early = jnp.pad(jnp.concatenate(pieces[:-1], axis=1), ((0, 0), (0, columns)))
    early, late = lax.optimization_barrier((early, pieces[-1]))
    return lax.dynamic_update_slice(early, late, (0, latents.shape[2] - columns))[None]


def solution(mesh):
    in_specs = (
        P(("group", "section"), None, ("span", "mp")),
        P(None, ("group", "section"), None, ("span", "mp")),
        P(("group", "section"), ("span", "mp"), None),
        P(("span", "mp"), None),
        P(),
        P(("group", "section")),
        P("group"),
    )
    out_specs = P(("group", "section"), ("span", "mp"), None)
    return jax.shard_map(shards, mesh=mesh, in_specs=in_specs, out_specs=out_specs, check_vma=False)
```

```python
import functools
import math

import jax
import jax.numpy as jnp
from jax import lax
from jax.experimental import pallas as pl
from jax.experimental.pallas import tpu as pltpu
from jax.sharding import PartitionSpec as P

HD = 128
CHUNKS = 4
NEG_BIG = -1e30
VMEM_LIMIT = 4 * 1024 * 1024


def scores_of(q, keys):
    return lax.dot_general(
        q, keys, (((1,), (1,)), ((), ())), preferred_element_type=jnp.float32
    )


FACTOR = math.log2(math.e) / math.sqrt(HD)


def exponentials(scores, top):
    wide = jnp.concatenate([top] * (scores.shape[1] // HD), axis=1)
    return jnp.exp2((scores - wide) * FACTOR).astype(jnp.bfloat16)


def own_kernel(q_ref, own_ref, acc_ref, den_ref, top_ref):
    rows, width = q_ref.shape
    ones = jnp.ones((own_ref.shape[2], HD), jnp.bfloat16)
    for h in range(width // HD):
        head = slice(h * HD, (h + 1) * HD)
        scores = scores_of(q_ref[:, head], own_ref[0, 0, :, head])
        top = jnp.broadcast_to(jnp.max(scores, axis=1, keepdims=True), (rows, HD))
        values = jnp.concatenate([own_ref[1, 0, :, head], ones], axis=1)
        both = jnp.dot(
            exponentials(scores, top), values, preferred_element_type=jnp.float32
        )
        acc_ref[:, head] = both[:, :HD]
        den_ref[:, head] = both[:, HD:]
        top_ref[:, head] = top


def halo_kernel(
    first, last, q_ref, halo_ref, mask_ref, acc_ref, den_ref, top_ref, *outs
):
    rows, width = outs[0].shape
    part = slice(first, first + rows)
    mask = mask_ref[...]
    ones = jnp.ones((halo_ref.shape[2], HD), jnp.bfloat16)
    heads = [slice(h * HD, (h + 1) * HD) for h in range(width // HD)]
    scores = [scores_of(q_ref[part, head], halo_ref[0, 0, :, head]) + mask for head in heads]
    peaks = [jnp.max(s, axis=1, keepdims=True) for s in scores]
    probs, fades = [], []
    for head, s, peak in zip(heads, scores, peaks):
        before = top_ref[part, head]
        top = jnp.maximum(before, jnp.broadcast_to(peak, before.shape))
        probs.append(exponentials(s, top))
        fades.append(jnp.exp2((before - top) * FACTOR))
        if not last:
            outs[2][:, head] = top
    for head, p, fade in zip(heads, probs, fades):
        values = jnp.concatenate([halo_ref[1, 0, :, head], ones], axis=1)
        both = jnp.dot(p, values, preferred_element_type=jnp.float32)
        weighted = acc_ref[part, head] * fade + both[:, :HD]
        total = den_ref[part, head] * fade + both[:, HD:]
        if last:
            outs[0][:, head] = (weighted / total).astype(outs[0].dtype)
        else:
            outs[0][:, head] = weighted
            outs[1][:, head] = total


VMEM_SPEC = pl.BlockSpec(memory_space=pltpu.VMEM)


def attend(kernel, name, out_shape, flops, *operands):
    return pl.pallas_call(
        kernel,
        out_shape=out_shape,
        in_specs=[VMEM_SPEC] * len(operands),
        out_specs=(VMEM_SPEC,) * len(out_shape),
        compiler_params=pltpu.CompilerParams(vmem_limit_bytes=VMEM_LIMIT),
        cost_estimate=pl.CostEstimate(
            flops=flops,
            bytes_accessed=sum(x.size * x.dtype.itemsize for x in operands),
            transcendentals=flops // (4 * HD),
        ),
        name=name,
    )(*operands)


def hold_kernel(src_ref, dst_ref, sem):
    copy = pltpu.make_async_copy(src_ref, dst_ref, sem)
    copy.start()
    copy.wait()


def hold(array):
    return pl.pallas_call(
        hold_kernel,
        out_shape=jax.ShapeDtypeStruct(array.shape, array.dtype),
        in_specs=[pl.BlockSpec(memory_space=pltpu.HBM)],
        out_specs=VMEM_SPEC,
        scratch_shapes=[pltpu.SemaphoreType.DMA],
        compiler_params=pltpu.CompilerParams(vmem_limit_bytes=VMEM_LIMIT),
        cost_estimate=pl.CostEstimate(flops=0, bytes_accessed=1024, transcendentals=0),
        name="hold",
    )(array)


def project_kernel(parts, rows, first, base, *refs):
    att, weights = refs[:parts], refs[parts : 2 * parts]
    outs = refs[2 * parts + (1 if base else 0) :]
    columns = outs[-1].shape[1]
    tile = math.gcd(columns, 256)
    for t in range(0, columns, tile):
        total = refs[2 * parts][:, t : t + tile] if base else None
        for a, w in zip(att, weights):
            term = jnp.dot(
                a[...], w[:, first + t : first + t + tile], preferred_element_type=jnp.float32
            )
            total = term if total is None else total + term
        if len(outs) == 1:
            outs[0][:, t : t + tile] = total
            continue
        for i, out in enumerate(outs):
            out[:, t : t + tile] = total[i * rows : (i + 1) * rows].astype(out.dtype)


def project(att, weights, base, rows, first, columns, split):
    parts = len(att)
    all_rows, depth = att[0].shape
    send = jax.ShapeDtypeStruct((rows, columns), jnp.bfloat16)
    keep = jax.ShapeDtypeStruct((rows, columns), jnp.float32)
    blocks = all_rows // rows
    whole = jax.ShapeDtypeStruct((all_rows, columns), jnp.float32)
    out_shape = (send,) * (blocks - 1) + (keep,) if split else (whole,)
    bases = [] if base is None else [base]
    return pl.pallas_call(
        functools.partial(project_kernel, parts, rows, first, len(bases)),
        out_shape=out_shape,
        in_specs=[VMEM_SPEC] * (2 * parts + len(bases)),
        out_specs=(VMEM_SPEC,) * len(out_shape),
        compiler_params=pltpu.CompilerParams(vmem_limit_bytes=VMEM_LIMIT),
        cost_estimate=pl.CostEstimate(
            flops=2 * parts * all_rows * depth * columns,
            bytes_accessed=2 * parts * depth * columns,
            transcendentals=0,
        ),
        name="project",
    )(*att, *weights, *bases)


def combine_kernel(first, latents_ref, gate_ref, keep_ref, *refs):
    others, out_ref = refs[:-1], refs[-1]
    part = slice(first, first + keep_ref.shape[1])
    total = keep_ref[...]
    for other in others:
        total += other[...].astype(jnp.float32)
    out_ref[...] = (
        latents_ref[:, part].astype(jnp.float32) + gate_ref[:, part] * total
    ).astype(out_ref.dtype)


def combine(latents, gate_row, keep, others, first):
    rows, columns = keep.shape
    return pl.pallas_call(
        functools.partial(combine_kernel, first),
        out_shape=jax.ShapeDtypeStruct((rows, columns), latents.dtype),
        in_specs=[VMEM_SPEC] * (3 + len(others)),
        out_specs=VMEM_SPEC,
        compiler_params=pltpu.CompilerParams(vmem_limit_bytes=VMEM_LIMIT),
        cost_estimate=pl.CostEstimate(
            flops=4 * rows * columns, bytes_accessed=12 * rows * columns, transcendentals=0
        ),
        name="combine",
    )(latents, gate_row, keep, *others)


def rotate(value, axis, steps):
    count = lax.axis_size(axis)
    return lax.ppermute(value, axis, [(i, (i + steps) % count) for i in range(count)])


def shards(queries, keys_values, latents, out_weight, gate_table, level_index, pair_window):
    sections, spans, cores = (lax.axis_size(a) for a in ("section", "span", "mp"))
    section_id = lax.axis_index("section")
    rows = latents.shape[1]
    final_pair = pair_window.shape[0] - 1
    prev_width = jnp.where(section_id > 0, pair_window[jnp.clip(section_id - 1, 0, final_pair)], 0)
    next_width = jnp.where(
        section_id < sections - 1, pair_window[jnp.clip(section_id, 0, final_pair)], 0
    )
    swaps = [
        [pair for i in range(odd, sections - 1, 2) for pair in ((i, i + 1), (i + 1, i))]
        for odd in (0, 1)
    ]
    first_halo, second_halo = (lax.ppermute(keys_values, "section", pairs) for pairs in swaps)
    weights = [hold(out_weight)]
    weights += [hold(rotate(out_weight, "mp", l)) for l in range(1, cores)]
    own_latents = latents[0]
    span_tok = queries.shape[1]
    span_id, core_id = lax.axis_index("span"), lax.axis_index("mp")
    blocks = queries[0].reshape(spans * cores, rows, -1)
    order = []
    for l in range(cores - 1, -1, -1):
        for k in range(spans - 1, -1, -1):
            block = (span_id + k) % spans * cores + (core_id + l) % cores
            order.append(lax.dynamic_index_in_dim(blocks, block, keepdims=False))
    own_queries = jnp.concatenate(order, axis=0)
    col = jnp.arange(span_tok, dtype=jnp.int32)[None]
    prev_keys, next_keys = col >= span_tok - prev_width, col < next_width
    from_next = section_id % 2 == 0
    first_mask = jnp.where(jnp.where(from_next, next_keys, prev_keys), 0.0, NEG_BIG)
    second_mask = jnp.where(jnp.where(from_next, prev_keys, next_keys), 0.0, NEG_BIG)

    gate_row = lax.dynamic_slice_in_dim(gate_table, level_index[0], 1, axis=0)
    width = queries.shape[2]
    wide = jax.ShapeDtypeStruct((span_tok, width), jnp.float32)
    flops = 4 * span_tok * span_tok * width
    state = attend(own_kernel, "attend_own", (wide,) * 3, flops, own_queries, keys_values)
    state, weights, gate_row = lax.optimization_barrier((state, weights, gate_row))
    kernel = functools.partial(halo_kernel, 0, False)
    state = attend(
        kernel, "attend_first", (wide,) * 3, flops, own_queries, first_halo, first_mask, *state
    )
    per_core = spans * rows
    out_shape = (jax.ShapeDtypeStruct((per_core, width), jnp.bfloat16),)
    att = []
    for l in range(cores - 1, -1, -1):
        kernel = functools.partial(halo_kernel, (cores - 1 - l) * per_core, True)
        (out,) = attend(
            kernel, "attend_second", out_shape, flops // cores,
            own_queries, second_halo, second_mask, *state,
        )
        att.insert(0, out if l == 0 else rotate(out, "mp", l))

    columns = latents.shape[2] // CHUNKS
    updates = []
    sends, keeps = [], []
    for c in range(CHUNKS):
        first = c * columns
        if c == 0:
            (base,) = project(att[:1], weights[:1], None, rows, first, columns, False)
            *send, keep = project(att[1:], weights[1:], base, rows, first, columns, True)
            att, keep = lax.optimization_barrier((att, keep))
        else:
            *send, keep = project(att, weights, None, rows, first, columns, True)
        sends.append(send)
        keeps.append(keep)
    sends[1], keeps[2] = lax.optimization_barrier((sends[1], keeps[2]))
    for c, (send, keep) in enumerate(zip(sends, keeps)):
        others = [rotate(send[spans - 1 - k], "span", k) for k in range(1, spans)]
        updates.append(combine(own_latents, gate_row, keep, others, c * columns))
    pieces = [rotate(update, "section", 1) for update in updates]
    early = jnp.pad(jnp.concatenate(pieces[:-1], axis=1), ((0, 0), (0, columns)))
    early, late = lax.optimization_barrier((early, pieces[-1]))
    return lax.dynamic_update_slice(early, late, (0, latents.shape[2] - columns))[None]


def solution(mesh):
    in_specs = (
        P(("group", "section"), None, ("span", "mp")),
        P(None, ("group", "section"), None, ("span", "mp")),
        P(("group", "section"), ("span", "mp"), None),
        P(("span", "mp"), None),
        P(),
        P(("group", "section")),
        P("group"),
    )
    out_specs = P(("group", "section"), ("span", "mp"), None)
    return jax.shard_map(shards, mesh=mesh, in_specs=in_specs, out_specs=out_specs, check_vma=False)
```

```python
import functools
import math

import jax
import jax.numpy as jnp
from jax import lax
from jax.experimental import pallas as pl
from jax.experimental.pallas import tpu as pltpu
from jax.sharding import PartitionSpec as P

HD = 128
CHUNKS = 4
NEG_BIG = -1e30
VMEM_LIMIT = 4 * 1024 * 1024


def scores_of(q, keys):
    return lax.dot_general(
        q, keys, (((1,), (1,)), ((), ())), preferred_element_type=jnp.float32
    )


FACTOR = math.log2(math.e) / math.sqrt(HD)


def exponentials(scores, top):
    wide = jnp.concatenate([top] * (scores.shape[1] // HD), axis=1)
    return jnp.exp2((scores - wide) * FACTOR).astype(jnp.bfloat16)


def own_kernel(q_ref, own_ref, acc_ref, den_ref, top_ref):
    rows, width = q_ref.shape
    ones = jnp.ones((own_ref.shape[2], HD), jnp.bfloat16)
    for h in range(width // HD):
        head = slice(h * HD, (h + 1) * HD)
        scores = scores_of(q_ref[:, head], own_ref[0, 0, :, head])
        top = jnp.broadcast_to(jnp.max(scores, axis=1, keepdims=True), (rows, HD))
        values = jnp.concatenate([own_ref[1, 0, :, head], ones], axis=1)
        both = jnp.dot(
            exponentials(scores, top), values, preferred_element_type=jnp.float32
        )
        acc_ref[:, head] = both[:, :HD]
        den_ref[:, head] = both[:, HD:]
        top_ref[:, head] = top


def halo_kernel(
    first, last, q_ref, halo_ref, mask_ref, acc_ref, den_ref, top_ref, *outs
):
    rows, width = outs[0].shape
    part = slice(first, first + rows)
    mask = mask_ref[...]
    heads = [slice(h * HD, (h + 1) * HD) for h in range(width // HD)]

    def visit():
        ones = jnp.ones((halo_ref.shape[2], HD), jnp.bfloat16)
        scores = [scores_of(q_ref[part, head], halo_ref[0, 0, :, head]) + mask for head in heads]
        peaks = [jnp.max(s, axis=1, keepdims=True) for s in scores]
        probs, fades = [], []
        for head, s, peak in zip(heads, scores, peaks):
            before = top_ref[part, head]
            top = jnp.maximum(before, jnp.broadcast_to(peak, before.shape))
            probs.append(exponentials(s, top))
            fades.append(jnp.exp2((before - top) * FACTOR))
            if not last:
                outs[2][:, head] = top
        for head, p, fade in zip(heads, probs, fades):
            values = jnp.concatenate([halo_ref[1, 0, :, head], ones], axis=1)
            both = jnp.dot(p, values, preferred_element_type=jnp.float32)
            weighted = acc_ref[part, head] * fade + both[:, :HD]
            total = den_ref[part, head] * fade + both[:, HD:]
            if last:
                outs[0][:, head] = (weighted / total).astype(outs[0].dtype)
            else:
                outs[0][:, head] = weighted
                outs[1][:, head] = total

    if not last:
        visit()
        return
    anything = jnp.max(mask) == 0.0
    pl.when(anything)(visit)

    @pl.when(jnp.logical_not(anything))
    def _():
        for head in heads:
            outs[0][:, head] = (acc_ref[part, head] / den_ref[part, head]).astype(outs[0].dtype)


VMEM_SPEC = pl.BlockSpec(memory_space=pltpu.VMEM)


def attend(kernel, name, out_shape, flops, *operands):
    return pl.pallas_call(
        kernel,
        out_shape=out_shape,
        in_specs=[VMEM_SPEC] * len(operands),
        out_specs=(VMEM_SPEC,) * len(out_shape),
        compiler_params=pltpu.CompilerParams(vmem_limit_bytes=VMEM_LIMIT),
        cost_estimate=pl.CostEstimate(
            flops=flops,
            bytes_accessed=sum(x.size * x.dtype.itemsize for x in operands),
            transcendentals=flops // (4 * HD),
        ),
        name=name,
    )(*operands)


def hold_kernel(src_ref, dst_ref, sem):
    copy = pltpu.make_async_copy(src_ref, dst_ref, sem)
    copy.start()
    copy.wait()


def hold(array):
    return pl.pallas_call(
        hold_kernel,
        out_shape=jax.ShapeDtypeStruct(array.shape, array.dtype),
        in_specs=[pl.BlockSpec(memory_space=pltpu.HBM)],
        out_specs=VMEM_SPEC,
        scratch_shapes=[pltpu.SemaphoreType.DMA],
        compiler_params=pltpu.CompilerParams(vmem_limit_bytes=VMEM_LIMIT),
        cost_estimate=pl.CostEstimate(flops=0, bytes_accessed=1024, transcendentals=0),
        name="hold",
    )(array)


def project_kernel(parts, rows, first, base, *refs):
    att, weights = refs[:parts], refs[parts : 2 * parts]
    outs = refs[2 * parts + (1 if base else 0) :]
    columns = outs[-1].shape[1]
    tile = math.gcd(columns, 256)
    for t in range(0, columns, tile):
        total = refs[2 * parts][:, t : t + tile] if base else None
        for a, w in zip(att, weights):
            term = jnp.dot(
                a[...], w[:, first + t : first + t + tile], preferred_element_type=jnp.float32
            )
            total = term if total is None else total + term
        if len(outs) == 1:
            outs[0][:, t : t + tile] = total
            continue
        for i, out in enumerate(outs):
            out[:, t : t + tile] = total[i * rows : (i + 1) * rows].astype(out.dtype)


def project(att, weights, base, rows, first, columns, split):
    parts = len(att)
    all_rows, depth = att[0].shape
    send = jax.ShapeDtypeStruct((rows, columns), jnp.bfloat16)
    keep = jax.ShapeDtypeStruct((rows, columns), jnp.float32)
    blocks = all_rows // rows
    whole = jax.ShapeDtypeStruct((all_rows, columns), jnp.float32)
    out_shape = (send,) * (blocks - 1) + (keep,) if split else (whole,)
    bases = [] if base is None else [base]
    return pl.pallas_call(
        functools.partial(project_kernel, parts, rows, first, len(bases)),
        out_shape=out_shape,
        in_specs=[VMEM_SPEC] * (2 * parts + len(bases)),
        out_specs=(VMEM_SPEC,) * len(out_shape),
        compiler_params=pltpu.CompilerParams(vmem_limit_bytes=VMEM_LIMIT),
        cost_estimate=pl.CostEstimate(
            flops=2 * parts * all_rows * depth * columns,
            bytes_accessed=2 * parts * depth * columns,
            transcendentals=0,
        ),
        name="project",
    )(*att, *weights, *bases)


def combine_kernel(first, latents_ref, gate_ref, keep_ref, *refs):
    others, out_ref = refs[:-1], refs[-1]
    part = slice(first, first + keep_ref.shape[1])
    total = keep_ref[...]
    for other in others:
        total += other[...].astype(jnp.float32)
    out_ref[...] = (
        latents_ref[:, part].astype(jnp.float32) + gate_ref[:, part] * total
    ).astype(out_ref.dtype)


def combine(latents, gate_row, keep, others, first):
    rows, columns = keep.shape
    return pl.pallas_call(
        functools.partial(combine_kernel, first),
        out_shape=jax.ShapeDtypeStruct((rows, columns), latents.dtype),
        in_specs=[VMEM_SPEC] * (3 + len(others)),
        out_specs=VMEM_SPEC,
        compiler_params=pltpu.CompilerParams(vmem_limit_bytes=VMEM_LIMIT),
        cost_estimate=pl.CostEstimate(
            flops=4 * rows * columns, bytes_accessed=12 * rows * columns, transcendentals=0
        ),
        name="combine",
    )(latents, gate_row, keep, *others)


def rotate(value, axis, steps):
    count = lax.axis_size(axis)
    return lax.ppermute(value, axis, [(i, (i + steps) % count) for i in range(count)])


def shards(queries, keys_values, latents, out_weight, gate_table, level_index, pair_window):
    sections, spans, cores = (lax.axis_size(a) for a in ("section", "span", "mp"))
    section_id = lax.axis_index("section")
    rows = latents.shape[1]
    final_pair = pair_window.shape[0] - 1
    prev_width = jnp.where(section_id > 0, pair_window[jnp.clip(section_id - 1, 0, final_pair)], 0)
    next_width = jnp.where(
        section_id < sections - 1, pair_window[jnp.clip(section_id, 0, final_pair)], 0
    )
    swaps = [
        [pair for i in range(odd, sections - 1, 2) for pair in ((i, i + 1), (i + 1, i))]
        for odd in (0, 1)
    ]
    first_halo, second_halo = (lax.ppermute(keys_values, "section", pairs) for pairs in swaps)
    weights = [hold(out_weight)]
    weights += [hold(rotate(out_weight, "mp", l)) for l in range(1, cores)]
    own_latents = latents[0]
    span_tok = queries.shape[1]
    span_id, core_id = lax.axis_index("span"), lax.axis_index("mp")
    blocks = queries[0].reshape(spans * cores, rows, -1)
    order = []
    for l in range(cores - 1, -1, -1):
        for k in range(spans - 1, -1, -1):
            block = (span_id + k) % spans * cores + (core_id + l) % cores
            order.append(lax.dynamic_index_in_dim(blocks, block, keepdims=False))
    own_queries = jnp.concatenate(order, axis=0)
    col = jnp.arange(span_tok, dtype=jnp.int32)[None]
    prev_keys, next_keys = col >= span_tok - prev_width, col < next_width
    from_next = section_id % 2 == 0
    first_mask = jnp.where(jnp.where(from_next, next_keys, prev_keys), 0.0, NEG_BIG)
    second_mask = jnp.where(jnp.where(from_next, prev_keys, next_keys), 0.0, NEG_BIG)

    gate_row = lax.dynamic_slice_in_dim(gate_table, level_index[0], 1, axis=0)
    width = queries.shape[2]
    wide = jax.ShapeDtypeStruct((span_tok, width), jnp.float32)
    flops = 4 * span_tok * span_tok * width
    state = attend(own_kernel, "attend_own", (wide,) * 3, flops, own_queries, keys_values)
    state, weights, gate_row = lax.optimization_barrier((state, weights, gate_row))
    kernel = functools.partial(halo_kernel, 0, False)
    state = attend(
        kernel, "attend_first", (wide,) * 3, flops, own_queries, first_halo, first_mask, *state
    )
    per_core = spans * rows
    out_shape = (jax.ShapeDtypeStruct((per_core, width), jnp.bfloat16),)
    att = []
    for l in range(cores - 1, -1, -1):
        kernel = functools.partial(halo_kernel, (cores - 1 - l) * per_core, True)
        (out,) = attend(
            kernel, "attend_second", out_shape, flops // cores,
            own_queries, second_halo, second_mask, *state,
        )
        att.insert(0, out if l == 0 else rotate(out, "mp", l))

    columns = latents.shape[2] // CHUNKS
    updates = []
    sends, keeps = [], []
    for c in range(CHUNKS):
        first = c * columns
        if c == 0:
            (base,) = project(att[:1], weights[:1], None, rows, first, columns, False)
            *send, keep = project(att[1:], weights[1:], base, rows, first, columns, True)
            att, keep = lax.optimization_barrier((att, keep))
        else:
            *send, keep = project(att, weights, None, rows, first, columns, True)
        sends.append(send)
        keeps.append(keep)
    sends[1], keeps[2] = lax.optimization_barrier((sends[1], keeps[2]))
    for c, (send, keep) in enumerate(zip(sends, keeps)):
        others = [rotate(send[spans - 1 - k], "span", k) for k in range(1, spans)]
        updates.append(combine(own_latents, gate_row, keep, others, c * columns))
    pieces = [rotate(update, "section", 1) for update in updates]
    early = jnp.pad(jnp.concatenate(pieces[:-1], axis=1), ((0, 0), (0, columns)))
    early, late = lax.optimization_barrier((early, pieces[-1]))
    return lax.dynamic_update_slice(early, late, (0, latents.shape[2] - columns))[None]


def solution(mesh):
    in_specs = (
        P(("group", "section"), None, ("span", "mp")),
        P(None, ("group", "section"), None, ("span", "mp")),
        P(("group", "section"), ("span", "mp"), None),
        P(("span", "mp"), None),
        P(),
        P(("group", "section")),
        P("group"),
    )
    out_specs = P(("group", "section"), ("span", "mp"), None)
    return jax.shard_map(shards, mesh=mesh, in_specs=in_specs, out_specs=out_specs, check_vma=False)
```

```python
import functools
import math

import jax
import jax.numpy as jnp
from jax import lax
from jax.experimental import pallas as pl
from jax.experimental.pallas import tpu as pltpu
from jax.sharding import PartitionSpec as P

HD = 128
CHUNKS = 4
NEG_BIG = -1e30
VMEM_LIMIT = 4 * 1024 * 1024


def scores_of(q, keys):
    return lax.dot_general(
        q, keys, (((1,), (1,)), ((), ())), preferred_element_type=jnp.float32
    )


FACTOR = math.log2(math.e) / math.sqrt(HD)


def exponentials(scores, top):
    wide = jnp.concatenate([top] * (scores.shape[1] // HD), axis=1)
    return jnp.exp2((scores - wide) * FACTOR).astype(jnp.bfloat16)


def own_kernel(q_ref, own_ref, acc_ref, den_ref, top_ref):
    rows, width = q_ref.shape
    ones = jnp.ones((own_ref.shape[2], HD), jnp.bfloat16)
    for h in range(width // HD):
        head = slice(h * HD, (h + 1) * HD)
        scores = scores_of(q_ref[:, head], own_ref[0, 0, :, head])
        top = jnp.broadcast_to(jnp.max(scores, axis=1, keepdims=True), (rows, HD))
        values = jnp.concatenate([own_ref[1, 0, :, head], ones], axis=1)
        both = jnp.dot(
            exponentials(scores, top), values, preferred_element_type=jnp.float32
        )
        acc_ref[:, head] = both[:, :HD]
        den_ref[:, head] = both[:, HD:]
        top_ref[:, head] = top


def halo_kernel(
    first, last, q_ref, halo_ref, mask_ref, acc_ref, den_ref, top_ref, *outs
):
    rows, width = outs[0].shape
    part = slice(first, first + rows)
    mask = mask_ref[...]
    ones = jnp.ones((halo_ref.shape[2], HD), jnp.bfloat16)
    heads = [slice(h * HD, (h + 1) * HD) for h in range(width // HD)]
    scores = [scores_of(q_ref[part, head], halo_ref[0, 0, :, head]) + mask for head in heads]
    peaks = [jnp.max(s, axis=1, keepdims=True) for s in scores]
    probs, fades = [], []
    for head, s, peak in zip(heads, scores, peaks):
        before = top_ref[part, head]
        top = jnp.maximum(before, jnp.broadcast_to(peak, before.shape))
        probs.append(exponentials(s, top))
        fades.append(jnp.exp2((before - top) * FACTOR))
        if not last:
            outs[2][:, head] = top
    for head, p, fade in zip(heads, probs, fades):
        values = jnp.concatenate([halo_ref[1, 0, :, head], ones], axis=1)
        both = jnp.dot(p, values, preferred_element_type=jnp.float32)
        weighted = acc_ref[part, head] * fade + both[:, :HD]
        total = den_ref[part, head] * fade + both[:, HD:]
        if last:
            outs[0][:, head] = (weighted / total).astype(outs[0].dtype)
        else:
            outs[0][:, head] = weighted
            outs[1][:, head] = total


VMEM_SPEC = pl.BlockSpec(memory_space=pltpu.VMEM)


def attend(kernel, name, out_shape, flops, *operands):
    return pl.pallas_call(
        kernel,
        out_shape=out_shape,
        in_specs=[VMEM_SPEC] * len(operands),
        out_specs=(VMEM_SPEC,) * len(out_shape),
        compiler_params=pltpu.CompilerParams(vmem_limit_bytes=VMEM_LIMIT),
        cost_estimate=pl.CostEstimate(
            flops=flops,
            bytes_accessed=sum(x.size * x.dtype.itemsize for x in operands),
            transcendentals=flops // (4 * HD),
        ),
        name=name,
    )(*operands)


def hold_kernel(src_ref, dst_ref, sem):
    copy = pltpu.make_async_copy(src_ref, dst_ref, sem)
    copy.start()
    copy.wait()


def hold(array):
    return pl.pallas_call(
        hold_kernel,
        out_shape=jax.ShapeDtypeStruct(array.shape, array.dtype),
        in_specs=[pl.BlockSpec(memory_space=pltpu.HBM)],
        out_specs=VMEM_SPEC,
        scratch_shapes=[pltpu.SemaphoreType.DMA],
        compiler_params=pltpu.CompilerParams(vmem_limit_bytes=VMEM_LIMIT),
        cost_estimate=pl.CostEstimate(flops=0, bytes_accessed=1024, transcendentals=0),
        name="hold",
    )(array)


def project_kernel(parts, rows, first, base, *refs):
    att, weights = refs[:parts], refs[parts : 2 * parts]
    outs = refs[2 * parts + (1 if base else 0) :]
    columns = outs[-1].shape[1]
    tile = math.gcd(columns, 256)
    for t in range(0, columns, tile):
        total = refs[2 * parts][:, t : t + tile] if base else None
        for a, w in zip(att, weights):
            term = jnp.dot(
                a[...], w[:, first + t : first + t + tile], preferred_element_type=jnp.float32
            )
            total = term if total is None else total + term
        if len(outs) == 1:
            outs[0][:, t : t + tile] = total
            continue
        for i, out in enumerate(outs):
            out[:, t : t + tile] = total[i * rows : (i + 1) * rows].astype(out.dtype)


def project(att, weights, base, rows, first, columns, split):
    parts = len(att)
    all_rows, depth = att[0].shape
    send = jax.ShapeDtypeStruct((rows, columns), jnp.bfloat16)
    keep = jax.ShapeDtypeStruct((rows, columns), jnp.float32)
    blocks = all_rows // rows
    whole = jax.ShapeDtypeStruct((all_rows, columns), jnp.float32)
    out_shape = (send,) * (blocks - 1) + (keep,) if split else (whole,)
    bases = [] if base is None else [base]
    return pl.pallas_call(
        functools.partial(project_kernel, parts, rows, first, len(bases)),
        out_shape=out_shape,
        in_specs=[VMEM_SPEC] * (2 * parts + len(bases)),
        out_specs=(VMEM_SPEC,) * len(out_shape),
        compiler_params=pltpu.CompilerParams(vmem_limit_bytes=VMEM_LIMIT),
        cost_estimate=pl.CostEstimate(
            flops=2 * parts * all_rows * depth * columns,
            bytes_accessed=2 * parts * depth * columns,
            transcendentals=0,
        ),
        name="project",
    )(*att, *weights, *bases)


def combine_kernel(first, latents_ref, gate_ref, keep_ref, *refs):
    others, out_ref = refs[:-1], refs[-1]
    part = slice(first, first + keep_ref.shape[1])
    total = keep_ref[...]
    for other in others:
        total += other[...].astype(jnp.float32)
    out_ref[...] = (
        latents_ref[:, part].astype(jnp.float32) + gate_ref[:, part] * total
    ).astype(out_ref.dtype)


def combine(latents, gate_row, keep, others, first):
    rows, columns = keep.shape
    return pl.pallas_call(
        functools.partial(combine_kernel, first),
        out_shape=jax.ShapeDtypeStruct((rows, columns), latents.dtype),
        in_specs=[VMEM_SPEC] * (3 + len(others)),
        out_specs=VMEM_SPEC,
        compiler_params=pltpu.CompilerParams(vmem_limit_bytes=VMEM_LIMIT),
        cost_estimate=pl.CostEstimate(
            flops=4 * rows * columns, bytes_accessed=12 * rows * columns, transcendentals=0
        ),
        name="combine",
    )(latents, gate_row, keep, *others)


def rotate(value, axis, steps):
    count = lax.axis_size(axis)
    return lax.ppermute(value, axis, [(i, (i + steps) % count) for i in range(count)])


def shards(queries, keys_values, latents, out_weight, gate_table, level_index, pair_window):
    sections, spans, cores = (lax.axis_size(a) for a in ("section", "span", "mp"))
    section_id = lax.axis_index("section")
    rows = latents.shape[1]
    final_pair = pair_window.shape[0] - 1
    prev_width = jnp.where(section_id > 0, pair_window[jnp.clip(section_id - 1, 0, final_pair)], 0)
    next_width = jnp.where(
        section_id < sections - 1, pair_window[jnp.clip(section_id, 0, final_pair)], 0
    )
    swaps = [
        [pair for i in range(odd, sections - 1, 2) for pair in ((i, i + 1), (i + 1, i))]
        for odd in (0, 1)
    ]
    first_halo, second_halo = (lax.ppermute(keys_values, "section", pairs) for pairs in swaps)
    weights = [out_weight]
    weights += [hold(rotate(out_weight, "mp", l)) for l in range(1, cores)]
    own_latents = latents[0]
    span_tok = queries.shape[1]
    span_id, core_id = lax.axis_index("span"), lax.axis_index("mp")
    blocks = queries[0].reshape(spans * cores, rows, -1)
    order = []
    for l in range(cores - 1, -1, -1):
        for k in range(spans - 1, -1, -1):
            block = (span_id + k) % spans * cores + (core_id + l) % cores
            order.append(lax.dynamic_index_in_dim(blocks, block, keepdims=False))
    own_queries = jnp.concatenate(order, axis=0)
    col = jnp.arange(span_tok, dtype=jnp.int32)[None]
    prev_keys, next_keys = col >= span_tok - prev_width, col < next_width
    from_next = section_id % 2 == 0
    first_mask = jnp.where(jnp.where(from_next, next_keys, prev_keys), 0.0, NEG_BIG)
    second_mask = jnp.where(jnp.where(from_next, prev_keys, next_keys), 0.0, NEG_BIG)

    gate_row = lax.dynamic_slice_in_dim(gate_table, level_index[0], 1, axis=0)
    width = queries.shape[2]
    wide = jax.ShapeDtypeStruct((span_tok, width), jnp.float32)
    flops = 4 * span_tok * span_tok * width
    state = attend(own_kernel, "attend_own", (wide,) * 3, flops, own_queries, keys_values)
    state, weights[1:], gate_row = lax.optimization_barrier((state, weights[1:], gate_row))
    kernel = functools.partial(halo_kernel, 0, False)
    state = attend(
        kernel, "attend_first", (wide,) * 3, flops, own_queries, first_halo, first_mask, *state
    )
    per_core = spans * rows
    out_shape = (jax.ShapeDtypeStruct((per_core, width), jnp.bfloat16),)
    att = []
    for l in range(cores - 1, -1, -1):
        kernel = functools.partial(halo_kernel, (cores - 1 - l) * per_core, True)
        (out,) = attend(
            kernel, "attend_second", out_shape, flops // cores,
            own_queries, second_halo, second_mask, *state,
        )
        att.insert(0, out if l == 0 else rotate(out, "mp", l))

    columns = latents.shape[2] // CHUNKS
    updates = []
    sends, keeps = [], []
    for c in range(CHUNKS):
        first = c * columns
        if c == 0:
            (base,) = project(att[:1], weights[:1], None, rows, first, columns, False)
            *send, keep = project(att[1:], weights[1:], base, rows, first, columns, True)
            att, keep = lax.optimization_barrier((att, keep))
        else:
            *send, keep = project(att, weights, None, rows, first, columns, True)
        sends.append(send)
        keeps.append(keep)
    sends[1], keeps[2] = lax.optimization_barrier((sends[1], keeps[2]))
    for c, (send, keep) in enumerate(zip(sends, keeps)):
        others = [rotate(send[spans - 1 - k], "span", k) for k in range(1, spans)]
        updates.append(combine(own_latents, gate_row, keep, others, c * columns))
    pieces = [rotate(update, "section", 1) for update in updates]
    early = jnp.pad(jnp.concatenate(pieces[:-1], axis=1), ((0, 0), (0, columns)))
    early, late = lax.optimization_barrier((early, pieces[-1]))
    return lax.dynamic_update_slice(early, late, (0, latents.shape[2] - columns))[None]


def solution(mesh):
    in_specs = (
        P(("group", "section"), None, ("span", "mp")),
        P(None, ("group", "section"), None, ("span", "mp")),
        P(("group", "section"), ("span", "mp"), None),
        P(("span", "mp"), None),
        P(),
        P(("group", "section")),
        P("group"),
    )
    out_specs = P(("group", "section"), ("span", "mp"), None)
    return jax.shard_map(shards, mesh=mesh, in_specs=in_specs, out_specs=out_specs, check_vma=False)
```
